256 devices in a mesh: snap: 64 (over z, y, core), rep: 4 (over x).
Axes of the slice: x: 4, y: 4, z: 8, core: 2. Of those that a mesh axis runs over, the one named last changes fastest.
Arguments:
- features: float32 [64, 8192, 256], P('snap', 'rep'), parts along dimension 1, may hold values from -6 to 6
- tiles: float32 [64, 128, 128, 128], P('snap', 'rep'), parts along dimension 1, may hold values from -0.375 to 0.375
- coords: int32 [64, 128, 2], P('snap', 'rep'), parts along dimension 1, may hold values from -1 to 15, as said below
- temporal: float32 [64, 64], replicated, may hold values from 0 to 2, as said below
- weight_one: float32 [256, 256], replicated, may hold values from -0.375 to 0.375
- weight_two: float32 [256, 256], replicated, may hold values from -0.375 to 0.375
Outputs:
- hidden_two: float32 [64, 8192, 256], P('snap', 'rep'), parts along dimension 1
The draws below stay inside these ranges and needn't reach their ends.
There are 4 independent parts, one for each index of `rep`. The reference program is written for one: setup_inputs(seed, part) draws one part's arguments, and reference() takes and returns one part's arrays. A program takes and returns all parts, laid end to end along the dimension named above; an argument that names none is the same for every part. Nothing has to cross between parts.
Inputs may be any that keep to these rules, and one draw needn't show every extreme that they name: `coords`: each snapshot lists at most 32 distinct tiles (row block, column block) in its first slots; the remaining slots hold -1 in both entries; some snapshot uses all 32 slots. `temporal`: zero above the diagonal.
All inputs are finite; a program needn't handle non-finite values.
Results may differ from the reference program's by a relative error of at most 0.0003.
Values sent between devices are 32-bit elements; how exact they have to be, the bound alone decides.
No kernel may reach another device: no remote copies, remote signals or barrier semaphores. Data moves between devices by JAX's collectives and lax.ppermute only.
A program may use at most 64 MiB of HBM per device.

```python
import jax
import jax.numpy as jnp
from jax import lax

VERT = 2048
FEAT = 256
TILE = 128
MAXT = 32
SNAPS = 64
NBLK = 16


def draw_coords(key, part):
    key = jax.random.fold_in(key, 3)
    key_order, key_count, key_top = jax.random.split(key, 3)

    def one_order(sub_key):
        return jax.random.permutation(sub_key, NBLK * NBLK)
    orders = jax.vmap(one_order)(jax.random.split(key_order, SNAPS))[:, :MAXT]
    raw = jax.random.randint(key_count, (SNAPS,), 0, 64)
    lowest = MAXT // 4
    used_count = lowest + (MAXT - lowest) * (raw * raw * raw) // 250047
    top_snap = jax.random.randint(key_top, (), 0, SNAPS)
    used_count = jnp.where(jnp.arange(SNAPS) == top_snap, MAXT, used_count)
    used_slot = jnp.arange(MAXT)[None, :] < used_count[:, None]
    row_index = jnp.where(used_slot, orders // NBLK, -1)
    col_index = jnp.where(used_slot, orders % NBLK, -1)
    return jnp.stack([row_index, col_index], -1).astype(jnp.int32)


def draw_temporal(key, part):
    key = jax.random.fold_in(key, 7)
    spread = jax.random.uniform(key, (SNAPS, SNAPS), jnp.float32, 0.5, 1.5)
    later = jnp.arange(SNAPS)[:, None]
    earlier = jnp.arange(SNAPS)[None, :]
    scaled = spread / jnp.sqrt((later + 1).astype(jnp.float32))
    return jnp.where(earlier <= later, scaled, 0.0).astype(jnp.float32)


def shard_levels(key, dims, cuts, least, top_value):
    def one(axis_at, parts):
        draws = jax.random.uniform(jax.random.fold_in(jax.random.fold_in(key, 6), axis_at), (parts,), jnp.float32, least / len(cuts), top_value / len(cuts))
        return jnp.repeat(jnp.exp(draws), dims[axis_at] // parts).reshape((-1,) + (1,) * (len(dims) - axis_at - 1))

    level = one(*cuts[0])
    for cut in cuts[1:]:
        level = level * one(*cut)
    return level


def normal_values(stream_key, shape, deviation, bound, pieces=(), kind=jnp.bfloat16):
    values = deviation * jax.random.normal(stream_key, shape, jnp.float32)
    if pieces:
        values = values * shard_levels(stream_key, shape, pieces, -0.22, 0.18)
    return jnp.clip(values, -bound, bound).astype(kind)


def setup_inputs(seed: int = 0, part: int = 0) -> dict:
    key_of = jax.random.split(jax.random.key(seed), 7)
    own_keys = jax.random.split(jax.random.fold_in(key_of[6], part), 7)
    features = normal_values(own_keys[0], (SNAPS, VERT, FEAT), 1.0, 6.0, ((0, 64),), jnp.float32)
    tiles = normal_values(own_keys[1], (SNAPS, MAXT, TILE, TILE), (2 * TILE) ** -0.5, 0.375, ((0, 64),), jnp.float32)
    coords = draw_coords(jax.random.fold_in(jax.random.fold_in(key_of[6], part), 71), part)
    temporal = draw_temporal(jax.random.fold_in(key_of[6], 71), part)
    weight_one = normal_values(key_of[4], (FEAT, FEAT), FEAT ** -0.5, 0.375, (), jnp.float32)
    weight_two = normal_values(key_of[5], (FEAT, FEAT), FEAT ** -0.5, 0.375, (), jnp.float32)
    return {"features": features, "tiles": tiles, "coords": coords, "temporal": temporal, "weight_one": weight_one, "weight_two": weight_two}


def snapshot_product(state, tile_vals, tile_coords):
    hblocks = state.reshape(NBLK, TILE, FEAT)
    is_used = tile_coords[:, 0] >= 0
    col_index = jnp.where(is_used, tile_coords[:, 1], 0).astype(jnp.int32)
    gathered = hblocks[col_index]
    products = jnp.einsum("kij,kjf->kif", tile_vals, gathered, precision=lax.Precision.HIGHEST)
    one_hot = (tile_coords[:, 0][None, :] == jnp.arange(NBLK, dtype=jnp.int32)[:, None]).astype(jnp.float32)
    summed = jnp.einsum("rk,kif->rif", one_hot, products, precision=lax.Precision.HIGHEST)
    return summed.reshape(VERT, FEAT)


def reference(features, tiles, coords, temporal, weight_one, weight_two):
    state = features
    for weight in (weight_one, weight_two):
        def per_snap(items):
            return snapshot_product(items[0], items[1], items[2])

        summed = lax.map(per_snap, (state, tiles, coords))
        projected = jnp.dot(summed.reshape(-1, FEAT), weight, precision=lax.Precision.HIGHEST).reshape(SNAPS, VERT, FEAT)
        state = jnp.tanh(jnp.einsum("ts,svf->tvf", temporal, projected, precision=lax.Precision.HIGHEST))
    return state
```

```python
import jax
import jax.numpy as jnp
from jax import lax
from jax.experimental import pallas as pl
from jax.experimental.pallas import tpu as pltpu
from jax.sharding import PartitionSpec as P

NZ, NY, NC = 8, 4, 2
NYC = NY * NC
SNAPS = NZ * NYC
VERT, FEAT, TILE = 2048, 256, 128
HALF = FEAT // 2
OWN = VERT // SNAPS
NBLK = VERT // TILE
BF, F32 = jnp.bfloat16, jnp.float32
PIECE = jax.ShapeDtypeStruct((8, OWN, HALF), F32)
PARAMS = pltpu.CompilerParams(vmem_limit_bytes=32 * 1024 * 1024)
VSPEC = pl.BlockSpec(memory_space=pltpu.VMEM)
SSPEC = pl.BlockSpec(memory_space=pltpu.SMEM)


def split(x):
    hi = x.astype(BF)
    return hi, (x - hi.astype(F32)).astype(BF)


def dot(a, b):
    return jnp.dot(a, b, preferred_element_type=F32)


def vertex_base(pos, k, j, m, sign):
    z = lax.rem(pos[0] + sign * k + NZ, NZ)
    y = lax.rem(pos[1] + sign * j + NY, NY)
    c = pos[2] + m - 2 * m * pos[2]
    return pl.multiple_of(((z * NY + y) * NC + c) * OWN, OWN)


def put_block(pair, row, value):
    hi, lo = split(value)
    blk = row // TILE
    off = row % TILE
    if not isinstance(off, int):
        off = pl.multiple_of(off, OWN)
    n = value.shape[0]
    both = jnp.concatenate([hi, lo], axis=1)
    pair[blk, pl.ds(off, n), :] = both
    pair[blk, pl.ds(off + TILE, n), :] = both


def tile_products(coords, tiles, pair, acc):
    acc[...] = jnp.zeros_like(acc)
    count = tiles.shape[0]
    for k in range(count):
        row = coords[2 * k]
        used = row >= 0
        row = jnp.where(used, row, NBLK)
        col = jnp.where(used, coords[2 * k + 1], 0)
        hi, lo = split(tiles[k])
        wide = dot(jnp.concatenate([hi, lo], axis=1), pair[col])
        acc[row] += wide[:, :HALF] + wide[:, HALF:]


def emit(pos, acc, outs, z_first):
    for a in range(8):
        for b in range(8):
            k, jm = (a, b) if z_first else (b, a)
            base = vertex_base(pos, k, jm // NC, jm % NC, 1)
            off = pl.multiple_of(base % TILE, OWN)
            outs[a][b] = acc[base // TILE, pl.ds(off, OWN), :]


def collect(pos, parts, pair, z_last):
    for a in range(8):
        for b in range(8):
            k, jm = (a, b) if z_last else (b, a)
            base = vertex_base(pos, k, jm // NC, jm % NC, -1)
            put_block(pair, base, parts[a][b])


def first_kernel(z_first, pos, coords, state, tiles, weight, *rest):
    outs, (pair, acc) = rest[:8], rest[8:]
    w_hi, w_lo = split(weight[...])
    for r in range(0, VERT, 256):
        s_hi, s_lo = split(state[r : r + 256, :])
        u = dot(s_hi, w_hi) + (dot(s_hi, w_lo) + dot(s_lo, w_hi))
        for q in range(0, 256, TILE):
            put_block(pair, r + q, u[q : q + TILE])
    tile_products(coords, tiles, pair, acc)
    emit(pos, acc, outs, z_first)


SCRATCH = [pltpu.VMEM((NBLK, 2 * TILE, FEAT), BF), pltpu.VMEM((NBLK + 1, TILE, HALF), F32)]


def cost(flops, moved):
    return pl.CostEstimate(flops=flops, bytes_accessed=moved, transcendentals=0)


def first_product(z_first, pos, coords, state, tiles, weight_half):
    def kernel(*refs):
        first_kernel(z_first, *refs)

    return pl.pallas_call(
        kernel,
        out_shape=[PIECE] * 8,
        in_specs=[SSPEC, SSPEC, VSPEC, VSPEC, VSPEC],
        out_specs=[VSPEC] * 8,
        scratch_shapes=SCRATCH,
        compiler_params=PARAMS,
        cost_estimate=cost(1_600_000_000, 5 << 20),
        name="first_product",
    )(pos, coords, state, tiles, weight_half)


def early_kernel(pos, coords, tiles, *rest):
    parts, out, (pair, acc) = rest[:8], rest[8], rest[9:]
    collect(pos, parts, pair, False)
    tile_products(coords, tiles, pair, acc)
    out[...] = acc[:NBLK].reshape(VERT, HALF)


def early_product(pos, coords, tiles, parts):
    return pl.pallas_call(
        early_kernel,
        out_shape=jax.ShapeDtypeStruct((VERT, HALF), F32),
        in_specs=[SSPEC, SSPEC, VSPEC] + [VSPEC] * 8,
        out_specs=VSPEC,
        scratch_shapes=SCRATCH,
        compiler_params=PARAMS,
        cost_estimate=cost(800_000_000, 4 << 20),
        name="early_product",
    )(pos, coords, tiles, *parts)


def project(acc_left, acc_right, weight, acc):
    w_hi, w_lo = split(weight[...])
    for r in range(0, NBLK, 2):
        x = jnp.concatenate(
            [acc_left[r * TILE : (r + 2) * TILE, :], acc_right[r * TILE : (r + 2) * TILE, :]], axis=1
        )
        x_hi, x_lo = split(x)
        u = dot(x_hi, w_hi) + (dot(x_hi, w_lo) + dot(x_lo, w_hi))
        acc[r] = u[:TILE]
        acc[r + 1] = u[TILE:]


def late_kernel(pos, coords, tiles, left, weight, *rest):
    parts, right, outs, (pair, acc) = rest[:8], rest[8], rest[9:17], rest[17:]
    collect(pos, parts, pair, True)
    tile_products(coords, tiles, pair, acc)
    right[...] = acc[:NBLK].reshape(VERT, HALF)
    project(left, right, weight, acc)
    emit(pos, acc, outs, True)


def late_product(pos, coords, tiles, left, weight_half, parts):
    res = pl.pallas_call(
        late_kernel,
        out_shape=[jax.ShapeDtypeStruct((VERT, HALF), F32)] + [PIECE] * 8,
        in_specs=[SSPEC, SSPEC] + [VSPEC] * 11,
        out_specs=[VSPEC] * 9,
        scratch_shapes=SCRATCH,
        compiler_params=PARAMS,
        cost_estimate=cost(1_600_000_000, 6 << 20),
        name="late_product",
    )(pos, coords, tiles, left, weight_half, *parts)
    return res[0], res[1:]


def project_kernel(pos, left, right, weight, *rest):
    outs, (acc,) = rest[:8], rest[8:]
    project(left, right, weight, acc)
    emit(pos, acc, outs, False)


def last_project(pos, left, right, weight_half):
    return pl.pallas_call(
        project_kernel,
        out_shape=[PIECE] * 8,
        in_specs=[SSPEC] + [VSPEC] * 3,
        out_specs=[VSPEC] * 8,
        scratch_shapes=[SCRATCH[1]],
        compiler_params=PARAMS,
        cost_estimate=cost(800_000_000, 3 << 20),
        name="last_project",
    )(pos, left, right, weight_half)


def mix_kernel(mixer, *rest):
    parts, outs = rest[:8], rest[8:]
    t_hi, t_lo = split(mixer[...])
    lhs = jnp.concatenate([t_hi, t_lo, t_hi, t_lo], axis=1)
    for i in range(0, OWN, 2):
        x = jnp.concatenate(
            [jnp.concatenate([p[:, i + q, :] for p in parts], axis=0) for q in range(2)], axis=1
        )
        hi, lo = split(x)
        h = jnp.tanh(dot(lhs, jnp.concatenate([hi, hi, lo, lo], axis=0)))
        for q in range(2):
            for a in range(8):
                outs[a][:, i + q, :] = h[8 * a : 8 * a + 8, q * HALF : (q + 1) * HALF]


def mix(mixer, parts):
    return pl.pallas_call(
        mix_kernel,
        out_shape=[PIECE] * 8,
        in_specs=[VSPEC] * 9,
        out_specs=[VSPEC] * 8,
        compiler_params=PARAMS,
        cost_estimate=cost(800_000_000, 2 << 20),
        name="mix",
    )(mixer, *parts)


def swap_kernel(*refs):
    ins, outs = refs[:8], refs[8:]
    for a in range(8):
        for b in range(8):
            outs[a][b] = ins[b][a]


def swap(parts):
    return pl.pallas_call(
        swap_kernel,
        out_shape=[PIECE] * 8,
        in_specs=[VSPEC] * 8,
        out_specs=[VSPEC] * 8,
        compiler_params=PARAMS,
        cost_estimate=cost(0, 2 << 20),
        name="swap",
    )(*parts)


def assemble_kernel(pos, *refs):
    early, late, out = refs[:8], refs[8:16], refs[16]
    for a in range(8):
        for b in range(8):
            base = vertex_base(pos, b, a // NC, a % NC, -1)
            out[pl.ds(base, OWN), :HALF] = early[a][b]
            base = vertex_base(pos, a, b // NC, b % NC, -1)
            out[pl.ds(base, OWN), HALF:] = late[a][b]


def assemble(pos, early, late):
    return pl.pallas_call(
        assemble_kernel,
        out_shape=jax.ShapeDtypeStruct((VERT, FEAT), F32),
        in_specs=[SSPEC] + [VSPEC] * 16,
        out_specs=VSPEC,
        compiler_params=PARAMS,
        cost_estimate=cost(0, 4 << 20),
        name="assemble",
    )(pos, *early, *late)


def moved(x, dz, dj, dm):
    pairs = []
    for s in range(SNAPS):
        z, y, c = s // NYC, s // NC % NY, s % NC
        pairs.append((s, ((z + dz) % NZ * NY + (y + dj) % NY) * NC + (c ^ dm)))
    return lax.ppermute(x, "snap", pairs)


ORDER = (1, 7, 2, 6, 3, 5, 4)


def along_z(parts):
    got = {k: moved(parts[k], k, 0, 0) for k in ORDER}
    got[0] = parts[0]
    return [got[k] for k in range(8)]


def along_y(parts):
    got = {a: moved(parts[a], 0, a // NC, a % NC) for a in (2, 6, 4, 3, 7, 5, 1)}
    got[0] = parts[0]
    return [got[a] for a in range(8)]


def shards(features, tiles, coords, temporal, weight_one, weight_two):
    me = lax.axis_index("snap")
    z, y, c = me // NYC, me // NC % NY, me % NC
    pos = jnp.stack([z, y, c]).astype(jnp.int32)
    state = features.reshape(VERT, FEAT)
    tiles = tiles.reshape(tiles.shape[1:])
    coords = coords.reshape(-1)

    ids = jnp.arange(SNAPS, dtype=jnp.int32)

    def places(sign, z_major):
        if z_major:
            k, jm = ids // NYC, ids % NYC
        else:
            k, jm = ids % NZ, ids // NZ
        j, m = jm // NC, jm % NC
        return ((z + sign * k) % NZ * NY + (y + sign * j) % NY) * NC + (c + m) % NC

    def mixer(rows, cols):
        left = (rows[:, None] == ids[None, :]).astype(F32)
        right = (cols[None, :] == ids[:, None]).astype(F32)
        high = lax.Precision.HIGHEST
        return jnp.dot(jnp.dot(left, temporal, precision=high), right, precision=high)

    mix_b = mixer(places(1, True), places(-1, False))
    mix_a = mixer(places(1, False), places(-1, True))

    b = first_product(True, pos, coords, state, tiles, weight_one[:, :HALF])
    a = first_product(False, pos, coords, state, tiles, weight_one[:, HALF:])
    for depth in range(2):
        b = along_y(swap(along_z(b)))
        a = along_z(swap(along_y(a)))
        b = mix(mix_b, b)
        a = mix(mix_a, a)
        b = along_y(swap(along_z(b)))
        a = along_z(swap(along_y(a)))
        if depth == 0:
            left = early_product(pos, coords, tiles, b)
            right, b = late_product(pos, coords, tiles, left, weight_two[:, :HALF], a)
            a = last_project(pos, left, right, weight_two[:, HALF:])
    return assemble(pos, b, a).reshape(features.shape)


def solution(mesh):
    return jax.shard_map(
        shards,
        mesh=mesh,
        in_specs=(
            P("snap", "rep", None),
            P("snap", "rep", None, None),
            P("snap", "rep", None),
            P(),
            P(),
            P(),
        ),
        out_specs=P("snap", "rep", None),
        check_vma=False,
    )
```

```python
import jax
import jax.numpy as jnp
from jax import lax
from jax.experimental import pallas as pl
from jax.experimental.pallas import tpu as pltpu
from jax.sharding import PartitionSpec as P

SNAPS = 64
VERT, FEAT, TILE = 2048, 256, 128
HALF = FEAT // 2
OWN = VERT // SNAPS
NBLK = VERT // TILE
BF, F32 = jnp.bfloat16, jnp.float32
WHOLE = jax.ShapeDtypeStruct((SNAPS, OWN, FEAT), F32)
PARAMS = pltpu.CompilerParams(vmem_limit_bytes=32 * 1024 * 1024)
VSPEC = pl.BlockSpec(memory_space=pltpu.VMEM)
SSPEC = pl.BlockSpec(memory_space=pltpu.SMEM)


def split(x):
    hi = x.astype(BF)
    return hi, (x - hi.astype(F32)).astype(BF)


def dot(a, b):
    return jnp.dot(a, b, preferred_element_type=F32)


def put_block(pair, row, value):
    hi, lo = split(value)
    blk = row // TILE
    both = jnp.concatenate([hi, lo], axis=1)
    pair[blk, :TILE] = both
    pair[blk, TILE:] = both


def tile_products(coords, tiles, pair, acc):
    acc[...] = jnp.zeros_like(acc)
    count = tiles.shape[0]
    for k in range(count):
        row = coords[2 * k]
        used = row >= 0
        row = jnp.where(used, row, NBLK)
        col = jnp.where(used, coords[2 * k + 1], 0)
        hi, lo = split(tiles[k])
        wide = dot(jnp.concatenate([hi, lo], axis=1), pair[col])
        acc[row] += wide[:, :HALF] + wide[:, HALF:]


def product_kernel(coords, state, tiles, weight, out, pair, acc):
    for h in range(2):
        cols = slice(h * HALF, (h + 1) * HALF)
        w_hi, w_lo = split(weight[:, cols])
        for r in range(0, VERT, 256):
            s_hi, s_lo = split(state[r : r + 256, :])
            u = dot(s_hi, w_hi) + (dot(s_hi, w_lo) + dot(s_lo, w_hi))
            for q in range(0, 256, TILE):
                put_block(pair, r + q, u[q : q + TILE])
        tile_products(coords, tiles, pair, acc)
        out[:, :, cols] = acc[:NBLK].reshape(SNAPS, OWN, HALF)


SCRATCH = [pltpu.VMEM((NBLK, 2 * TILE, FEAT), BF), pltpu.VMEM((NBLK + 1, TILE, HALF), F32)]


def cost(flops, moved):
    return pl.CostEstimate(flops=flops, bytes_accessed=moved, transcendentals=0)


def call(kernel, name, out_shape, in_specs, scratch, flops, moved, *args):
    return pl.pallas_call(
        kernel,
        out_shape=out_shape,
        in_specs=in_specs,
        out_specs=jax.tree.map(lambda _: VSPEC, out_shape),
        scratch_shapes=scratch,
        compiler_params=PARAMS,
        cost_estimate=cost(flops, moved),
        name=name,
    )(*args)


def product(coords, state, tiles, weight):
    return call(
        product_kernel, "product", WHOLE, [SSPEC, VSPEC, VSPEC, VSPEC], SCRATCH,
        3_200_000_000, 6 << 20, coords, state, tiles, weight,
    )


def mix_kernel(mixer, part, out):
    t_hi, t_lo = split(mixer[...])
    lhs = jnp.concatenate([t_hi, t_lo, t_hi, t_lo], axis=1)
    for i in range(OWN):
        hi, lo = split(part[:, i, :])
        out[:, i, :] = jnp.tanh(dot(lhs, jnp.concatenate([hi, hi, lo, lo], axis=0)))


def mix(mixer, part):
    return call(mix_kernel, "mix", WHOLE, [VSPEC] * 2, [], 1_600_000_000, 4 << 20, mixer, part)


def exchange(x):
    return lax.all_to_all(x, "snap", split_axis=0, concat_axis=0, tiled=True)


def shards(features, tiles, coords, temporal, weight_one, weight_two):
    tiles = tiles.reshape(tiles.shape[1:])
    coords = coords.reshape(-1)
    state = features
    for weight in (weight_one, weight_two):
        mine = product(coords, state.reshape(VERT, FEAT), tiles, weight)
        state = exchange(mix(temporal, exchange(mine)))
    return state.reshape(features.shape)


def solution(mesh):
    return jax.shard_map(
        shards,
        mesh=mesh,
        in_specs=(
            P("snap", "rep", None),
            P("snap", "rep", None, None),
            P("snap", "rep", None),
            P(),
            P(),
            P(),
        ),
        out_specs=P("snap", "rep", None),
        check_vma=False,
    )
```

```python
import jax
import jax.numpy as jnp
from jax import lax
from jax.experimental import pallas as pl
from jax.experimental.pallas import tpu as pltpu
from jax.sharding import PartitionSpec as P

NZ, NYC = 8, 8
SNAPS = NZ * NYC
VERT, FEAT, TILE = 2048, 256, 128
HALF = FEAT // 2
OWN = VERT // SNAPS
PLANE = NYC * OWN
NBLK = VERT // TILE
BF, F32 = jnp.bfloat16, jnp.float32
LIST = [jax.ShapeDtypeStruct((NYC, OWN, HALF), F32)] * NZ
GRID = jax.ShapeDtypeStruct((NYC, NZ, OWN, HALF), F32)
FLAT = jax.ShapeDtypeStruct((VERT, HALF), F32)
PARAMS = pltpu.CompilerParams(vmem_limit_bytes=32 * 1024 * 1024)
VSPEC = pl.BlockSpec(memory_space=pltpu.VMEM)
SSPEC = pl.BlockSpec(memory_space=pltpu.SMEM)


def split(x):
    hi = x.astype(BF)
    return hi, (x - hi.astype(F32)).astype(BF)


def dot(a, b):
    return jnp.dot(a, b, preferred_element_type=F32)


def put_block(pair, blk, value):
    hi, lo = split(value)
    both = jnp.concatenate([hi, lo], axis=1)
    pair[blk, :TILE] = both
    pair[blk, TILE:] = both


def tile_products(coords, tiles, pair, acc):
    acc[...] = jnp.zeros_like(acc)
    count = tiles.shape[0]
    for k in range(count):
        row = coords[2 * k]
        used = row >= 0
        row = jnp.where(used, row, NBLK)
        col = jnp.where(used, coords[2 * k + 1], 0)
        hi, lo = split(tiles[k])
        wide = dot(jnp.concatenate([hi, lo], axis=1), pair[col])
        acc[row] += wide[:, :HALF] + wide[:, HALF:]


SCRATCH = [pltpu.VMEM((NBLK, 2 * TILE, FEAT), BF), pltpu.VMEM((NBLK + 1, TILE, HALF), F32)]


def cost(flops, moved):
    return pl.CostEstimate(flops=flops, bytes_accessed=moved, transcendentals=0)


def call(kernel, name, out_shape, in_specs, scratch, flops, moved, *args):
    return pl.pallas_call(
        kernel,
        out_shape=out_shape,
        in_specs=in_specs,
        out_specs=jax.tree.map(lambda _: VSPEC, out_shape),
        scratch_shapes=scratch,
        compiler_params=PARAMS,
        cost_estimate=cost(flops, moved),
        name=name,
    )(*args)


def ahead(pos, k):
    return lax.rem(pos[0] + k, NZ)


def behind(pos, k):
    return lax.rem(pos[0] + NZ - k, NZ)


def emit_list(pos, acc, outs):
    for k in range(NZ):
        z = ahead(pos, k)
        outs[k][: NYC // 2] = acc[2 * z].reshape(NYC // 2, OWN, HALF)
        outs[k][NYC // 2 :] = acc[2 * z + 1].reshape(NYC // 2, OWN, HALF)


def emit_grid(pos, acc, out):
    for k in range(NZ):
        z = ahead(pos, k)
        out[: NYC // 2, k] = acc[2 * z].reshape(NYC // 2, OWN, HALF)
        out[NYC // 2 :, k] = acc[2 * z + 1].reshape(NYC // 2, OWN, HALF)


def put_plane(pair, z, value):
    flat = value.reshape(PLANE, HALF)
    put_block(pair, 2 * z, flat[:TILE])
    put_block(pair, 2 * z + 1, flat[TILE:])


def weigh_state(state, weight, pair):
    w_hi, w_lo = split(weight[...])
    for r in range(0, VERT, PLANE):
        s_hi, s_lo = split(state[r : r + PLANE, :])
        u = dot(s_hi, w_hi) + (dot(s_hi, w_lo) + dot(s_lo, w_hi))
        put_block(pair, r // TILE, u[:TILE])
        put_block(pair, r // TILE + 1, u[TILE:])


def first_list_kernel(pos, coords, state, tiles, weight, *rest):
    outs, (pair, acc) = rest[:NZ], rest[NZ:]
    weigh_state(state, weight, pair)
    tile_products(coords, tiles, pair, acc)
    emit_list(pos, acc, outs)


def first_grid_kernel(pos, coords, state, tiles, weight, out, pair, acc):
    weigh_state(state, weight, pair)
    tile_products(coords, tiles, pair, acc)
    emit_grid(pos, acc, out)


def first_list(*args):
    specs = [SSPEC, SSPEC, VSPEC, VSPEC, VSPEC]
    return call(first_list_kernel, "first_list", LIST, specs, SCRATCH, 1_600_000_000, 5 << 20, *args)


def first_grid(*args):
    specs = [SSPEC, SSPEC, VSPEC, VSPEC, VSPEC]
    return call(first_grid_kernel, "first_grid", GRID, specs, SCRATCH, 1_600_000_000, 5 << 20, *args)


def early_kernel(pos, coords, tiles, part, out, pair, acc):
    for k in range(NZ):
        put_plane(pair, behind(pos, k), part[:, k])
    tile_products(coords, tiles, pair, acc)
    out[...] = acc[:NBLK].reshape(VERT, HALF)


def early_product(*args):
    specs = [SSPEC, SSPEC, VSPEC, VSPEC]
    return call(early_kernel, "early_product", FLAT, specs, SCRATCH, 800_000_000, 4 << 20, *args)


def project(left, right, weight, acc):
    w_hi, w_lo = split(weight[...])
    for r in range(0, VERT, PLANE):
        x = jnp.concatenate([left[r : r + PLANE, :], right[r : r + PLANE, :]], axis=1)
        x_hi, x_lo = split(x)
        u = dot(x_hi, w_hi) + (dot(x_hi, w_lo) + dot(x_lo, w_hi))
        acc[r // TILE] = u[:TILE]
        acc[r // TILE + 1] = u[TILE:]


def late_kernel(pos, coords, tiles, left, weight, *rest):
    parts, right, outs, (pair, acc) = rest[:NZ], rest[NZ], rest[NZ + 1 : 2 * NZ + 1], rest[2 * NZ + 1 :]
    for k in range(NZ):
        put_plane(pair, behind(pos, k), parts[k][...])
    tile_products(coords, tiles, pair, acc)
    right[...] = acc[:NBLK].reshape(VERT, HALF)
    project(left, right, weight, acc)
    emit_list(pos, acc, outs)


def late_product(pos, coords, tiles, left, weight_half, parts):
    specs = [SSPEC, SSPEC] + [VSPEC] * (3 + NZ)
    res = call(
        late_kernel, "late_product", [FLAT] + LIST, specs, SCRATCH,
        1_600_000_000, 6 << 20, pos, coords, tiles, left, weight_half, *parts,
    )
    return res[0], res[1:]


def last_kernel(pos, left, right, weight, out, acc):
    project(left, right, weight, acc)
    emit_grid(pos, acc, out)


def last_project(*args):
    specs = [SSPEC] + [VSPEC] * 3
    return call(last_kernel, "last_project", GRID, specs, SCRATCH[1:], 800_000_000, 3 << 20, *args)


def mix_rows(mixer, load, store):
    t_hi, t_lo = split(mixer[...])
    lhs = jnp.concatenate([t_hi, t_lo, t_hi, t_lo], axis=1)
    for i in range(0, OWN, 2):
        hi, lo = split(jnp.concatenate([load(i), load(i + 1)], axis=1))
        h = jnp.tanh(dot(lhs, jnp.concatenate([hi, hi, lo, lo], axis=0)))
        store(i, h[:, :HALF])
        store(i + 1, h[:, HALF:])


def mix_to_list_kernel(mixer, part, *outs):
    def load(i):
        return jnp.concatenate([part[a, :, i, :] for a in range(NYC)], axis=0)

    def store(i, h):
        for k in range(NZ):
            outs[k][:, i, :] = h[NYC * k : NYC * k + NYC]

    mix_rows(mixer, load, store)


def mix_to_grid_kernel(mixer, *refs):
    parts, out = refs[:NZ], refs[NZ]

    def load(i):
        return jnp.concatenate([p[:, i, :] for p in parts], axis=0)

    def store(i, h):
        for a in range(NYC):
            out[a, :, i, :] = h[NZ * a : NZ * a + NZ]

    mix_rows(mixer, load, store)


def mix_to_list(mixer, part):
    return call(mix_to_list_kernel, "mix_to_list", LIST, [VSPEC] * 2, [], 800_000_000, 2 << 20, mixer, part)


def mix_to_grid(mixer, parts):
    return call(
        mix_to_grid_kernel, "mix_to_grid", GRID, [VSPEC] * (1 + NZ), [], 800_000_000, 2 << 20, mixer, *parts
    )


def join_kernel(*refs):
    for k in range(NZ):
        refs[NZ][:, k] = refs[k][...]


def join(parts):
    return call(join_kernel, "join", GRID, [VSPEC] * NZ, [], 0, 2 << 20, *parts)


def part_kernel(part, *outs):
    for k in range(NZ):
        outs[k][...] = part[:, k]


def separate(part):
    return call(part_kernel, "separate", LIST, [VSPEC], [], 0, 2 << 20, part)


def assemble_kernel(pos, left, *refs):
    right, out = refs[:NZ], refs[NZ]
    for k in range(NZ):
        rows = pl.ds(pl.multiple_of(behind(pos, k) * PLANE, PLANE), PLANE)
        out[rows, :HALF] = left[:, k].reshape(PLANE, HALF)
        out[rows, HALF:] = right[k][...].reshape(PLANE, HALF)


def assemble(pos, left, right):
    shape = jax.ShapeDtypeStruct((VERT, FEAT), F32)
    return call(assemble_kernel, "assemble", shape, [SSPEC] + [VSPEC] * (1 + NZ), [], 0, 4 << 20, pos, left, *right)


ORDER = (1, 7, 2, 6, 3, 5, 4)
GROUPS = [[z * NYC + a for a in range(NYC)] for z in range(NZ)]


def along_z(parts):
    got = [parts[0]] * NZ
    for k in ORDER:
        got[k] = lax.ppermute(parts[k], "snap", [(s, (s + k * NYC) % SNAPS) for s in range(SNAPS)])
    return got


def along_y(x):
    return lax.all_to_all(x, "snap", 0, 0, tiled=True, axis_index_groups=GROUPS)


def shards(features, tiles, coords, temporal, weight_one, weight_two):
    z = lax.axis_index("snap") // NYC
    pos = z.astype(jnp.int32).reshape(1)
    state = features.reshape(VERT, FEAT)
    tiles = tiles.reshape(tiles.shape[1:])
    coords = coords.reshape(-1)
    ids = jnp.arange(SNAPS, dtype=jnp.int32)

    def places(sign, z_major):
        k, a = (ids // NYC, ids % NYC) if z_major else (ids % NZ, ids // NZ)
        return (z + sign * k + NZ) % NZ * NYC + a

    def mixer(rows, cols):
        left = (rows[:, None] == ids[None, :]).astype(F32)
        right = (cols[None, :] == ids[:, None]).astype(F32)
        high = lax.Precision.HIGHEST
        return jnp.dot(jnp.dot(left, temporal, precision=high), right, precision=high)

    mix_b = mixer(places(1, True), places(-1, False))
    mix_a = mixer(places(1, False), places(-1, True))

    b = first_list(pos, coords, state, tiles, weight_one[:, :HALF])
    a = first_grid(pos, coords, state, tiles, weight_one[:, HALF:])
    for depth in range(2):
        b = along_y(join(along_z(b)))
        a = along_z(separate(along_y(a)))
        b = mix_to_list(mix_b, b)
        a = mix_to_grid(mix_a, a)
        b = along_y(join(along_z(b)))
        a = along_z(separate(along_y(a)))
        if depth == 0:
            left = early_product(pos, coords, tiles, b)
            right, b = late_product(pos, coords, tiles, left, weight_two[:, :HALF], a)
            a = last_project(pos, left, right, weight_two[:, HALF:])
    return assemble(pos, b, a).reshape(features.shape)


def solution(mesh):
    return jax.shard_map(
        shards,
        mesh=mesh,
        in_specs=(
            P("snap", "rep", None),
            P("snap", "rep", None, None),
            P("snap", "rep", None),
            P(),
            P(),
            P(),
        ),
        out_specs=P("snap", "rep", None),
        check_vma=False,
    )
```

```python
import jax
import jax.numpy as jnp
from jax import lax
from jax.experimental import pallas as pl
from jax.experimental.pallas import tpu as pltpu
from jax.sharding import PartitionSpec as P

NZ, NYC = 8, 8
SNAPS = NZ * NYC
ORDER = [z * NYC + a for a in range(NYC) for z in range(NZ)]
VERT, FEAT, TILE = 2048, 256, 128
HALF = FEAT // 2
OWN = VERT // SNAPS
NBLK = VERT // TILE
BF, F32 = jnp.bfloat16, jnp.float32
WHOLE = jax.ShapeDtypeStruct((SNAPS, OWN, FEAT), F32)
PARAMS = pltpu.CompilerParams(vmem_limit_bytes=32 << 20)
MOST = pltpu.CompilerParams(vmem_limit_bytes=60 << 20)
VSPEC = pl.BlockSpec(memory_space=pltpu.VMEM)
SSPEC = pl.BlockSpec(memory_space=pltpu.SMEM)
FAR = pl.BlockSpec(memory_space=pl.ANY)


def split(x):
    hi = x.astype(BF)
    return hi, (x - hi.astype(F32)).astype(BF)


def dot(a, b):
    return jnp.dot(a, b, preferred_element_type=F32)


def put_block(pair, h, blk, value):
    hi, lo = split(value)
    both = jnp.concatenate([hi, lo], axis=1)
    pair[h, blk, :TILE] = both
    pair[h, blk, TILE:] = both


def weigh_rows(rows, w_split, pair, r):
    w_hi, w_lo = w_split
    s_hi, s_lo = split(rows)
    u = dot(s_hi, w_hi) + (dot(s_hi, w_lo) + dot(s_lo, w_hi))
    for q in range(0, rows.shape[0], TILE):
        for h in range(2):
            put_block(pair, h, (r + q) // TILE, u[q : q + TILE, h * HALF : (h + 1) * HALF])


def add_tile(coords, k, tile, pair, acc):
    row = coords[0, k]
    used = row >= 0
    row = jnp.where(used, row, NBLK)
    col = jnp.where(used, coords[1, k], 0)
    lhs = jnp.concatenate(split(tile), axis=1)
    for h in range(2):
        wide = dot(lhs, pair[h, col])
        acc[row, :, h * HALF : (h + 1) * HALF] += wide[:, :HALF] + wide[:, HALF:]


def finish(acc, out):
    out[...] = acc[:NBLK].reshape(SNAPS, OWN, FEAT)


def product_kernel(coords, state, tiles, weight, out, pair, acc):
    w_split = split(weight[...])
    acc[...] = jnp.zeros_like(acc)
    for r in range(0, VERT, CHUNK):
        weigh_rows(state[r : r + CHUNK, :], w_split, pair, r)
    for k in range(tiles.shape[0]):
        add_tile(coords, k, tiles[k], pair, acc)
    finish(acc, out)


def loading_kernel(coords, state_far, tiles_far, weight_far, out, pair, acc, state, tiles, weight, sems):
    count = tiles.shape[0]
    step = count // PIECES
    copies = [pltpu.make_async_copy(weight_far, weight, sems.at[0])]
    for i in range(VERT // CHUNK):
        rows = pl.ds(i * CHUNK, CHUNK)
        copies.append(pltpu.make_async_copy(state_far.at[rows], state.at[rows], sems.at[len(copies)]))
    for i in range(PIECES):
        part = pl.ds(i * step, step)
        copies.append(pltpu.make_async_copy(tiles_far.at[part], tiles.at[part], sems.at[len(copies)]))
    for copy in copies:
        copy.start()
    acc[...] = jnp.zeros_like(acc)
    copies[0].wait()
    w_split = split(weight[...])
    for i in range(VERT // CHUNK):
        copies[1 + i].wait()
        weigh_rows(state[i * CHUNK : (i + 1) * CHUNK, :], w_split, pair, i * CHUNK)
    for i in range(PIECES):
        copies[1 + VERT // CHUNK + i].wait()
        for k in range(i * step, (i + 1) * step):
            add_tile(coords, k, tiles[k], pair, acc)
    finish(acc, out)


CHUNK, PIECES = 256, 4
SCRATCH = [pltpu.VMEM((2, NBLK, 2 * TILE, FEAT), BF), pltpu.VMEM((NBLK + 1, TILE, FEAT), F32)]


def cost(flops, moved):
    return pl.CostEstimate(flops=flops, bytes_accessed=moved, transcendentals=0)


def call(kernel, name, out_shape, in_specs, scratch, flops, moved, *args, params=PARAMS):
    return pl.pallas_call(
        kernel,
        out_shape=out_shape,
        in_specs=in_specs,
        out_specs=jax.tree.map(lambda _: VSPEC, out_shape),
        scratch_shapes=scratch,
        compiler_params=params,
        cost_estimate=cost(flops, moved),
        name=name,
    )(*args)


def product(coords, state, tiles, weight):
    return call(
        product_kernel, "product", WHOLE, [SSPEC, VSPEC, VSPEC, VSPEC], SCRATCH,
        3_200_000_000, 6 << 20, coords, state, tiles, weight,
    )


def loading_product(coords, state, tiles, weight):
    near = [pltpu.VMEM(x.shape, F32) for x in (state, tiles, weight)]
    sems = [pltpu.SemaphoreType.DMA((1 + VERT // CHUNK + PIECES,))]
    return call(
        loading_kernel, "loading_product", WHOLE, [SSPEC, FAR, FAR, FAR], SCRATCH + near + sems,
        3_200_000_000, 6 << 20, coords, state, tiles, weight, params=MOST,
    )


def mix_kernel(mixer, part, out):
    place = lax.broadcasted_iota(jnp.int32, (SNAPS, SNAPS), 0)
    snap = lax.broadcasted_iota(jnp.int32, (SNAPS, SNAPS), 1)
    pick = (lax.rem(place, NZ) * NYC + lax.div(place, NZ) == snap).astype(F32).astype(BF)

    def reorder(t):
        rows = dot(pick, t).astype(BF)
        return lax.dot_general(rows, pick, (((1,), (1,)), ((), ())), preferred_element_type=F32).astype(BF)

    t_hi, t_lo = [reorder(t) for t in split(mixer[...])]
    lhs = jnp.concatenate([t_hi, t_lo, t_hi, t_lo], axis=1)
    for h in range(2):
        cols = slice(h * HALF, (h + 1) * HALF)
        for i in range(0, OWN, 2):
            hi, lo = split(jnp.concatenate([part[:, i, cols], part[:, i + 1, cols]], axis=1))
            mixed = jnp.tanh(dot(lhs, jnp.concatenate([hi, hi, lo, lo], axis=0)))
            out[:, i, cols] = mixed[:, :HALF]
            out[:, i + 1, cols] = mixed[:, HALF:]


def mix(mixer, part):
    return call(mix_kernel, "mix", WHOLE, [VSPEC] * 2, [], 1_600_000_000, 4 << 20, mixer, part)


def exchange(x):
    return lax.all_to_all(x, "snap", split_axis=0, concat_axis=0, tiled=True, axis_index_groups=[ORDER])


def shards(features, tiles, coords, temporal, weight_one, weight_two):
    tiles = tiles.reshape(tiles.shape[1:])
    coords = coords[0].T
    mine = loading_product(coords, features.reshape(VERT, FEAT), tiles, weight_one)
    state = exchange(mix(temporal, exchange(mine)))
    mine = product(coords, state.reshape(VERT, FEAT), tiles, weight_two)
    return exchange(mix(temporal, exchange(mine))).reshape(features.shape)


def solution(mesh):
    return jax.shard_map(
        shards,
        mesh=mesh,
        in_specs=(
            P("snap", "rep", None),
            P("snap", "rep", None, None),
            P("snap", "rep", None),
            P(),
            P(),
            P(),
        ),
        out_specs=P("snap", "rep", None),
        check_vma=False,
    )
```

```python
import jax
import jax.numpy as jnp
from jax import lax
from jax.experimental import pallas as pl
from jax.experimental.pallas import tpu as pltpu
from jax.sharding import PartitionSpec as P

SNAPS = 64
VERT, FEAT, TILE = 2048, 256, 128
HALF = FEAT // 2
OWN = VERT // SNAPS
NBLK = VERT // TILE
BF, F32 = jnp.bfloat16, jnp.float32
WHOLE = jax.ShapeDtypeStruct((SNAPS, OWN, FEAT), F32)
PARAMS = pltpu.CompilerParams(vmem_limit_bytes=32 << 20)
MOST = pltpu.CompilerParams(vmem_limit_bytes=60 << 20)
VSPEC = pl.BlockSpec(memory_space=pltpu.VMEM)
SSPEC = pl.BlockSpec(memory_space=pltpu.SMEM)
FAR = pl.BlockSpec(memory_space=pl.ANY)


def split(x):
    hi = x.astype(BF)
    return hi, (x - hi.astype(F32)).astype(BF)


def dot(a, b):
    return jnp.dot(a, b, preferred_element_type=F32)


def put_block(pair, h, blk, value):
    hi, lo = split(value)
    both = jnp.concatenate([hi, lo], axis=1)
    pair[h, blk, :TILE] = both
    pair[h, blk, TILE:] = both


def weigh_rows(rows, w_split, pair, r):
    w_hi, w_lo = w_split
    s_hi, s_lo = split(rows)
    u = dot(s_hi, w_hi) + (dot(s_hi, w_lo) + dot(s_lo, w_hi))
    for q in range(0, rows.shape[0], TILE):
        for h in range(2):
            put_block(pair, h, (r + q) // TILE, u[q : q + TILE, h * HALF : (h + 1) * HALF])


def add_tile(coords, k, tile, pair, acc):
    row = coords[0, k]
    used = row >= 0
    row = jnp.where(used, row, NBLK)
    col = jnp.where(used, coords[1, k], 0)
    lhs = jnp.concatenate(split(tile), axis=1)
    for h in range(2):
        wide = dot(lhs, pair[h, col])
        acc[row, :, h * HALF : (h + 1) * HALF] += wide[:, :HALF] + wide[:, HALF:]


def finish(acc, out):
    out[...] = acc[:NBLK].reshape(SNAPS, OWN, FEAT)


def product_kernel(coords, state, tiles, weight, out, pair, acc):
    w_split = split(weight[...])
    acc[...] = jnp.zeros_like(acc)
    for r in range(0, VERT, CHUNK):
        weigh_rows(state[r : r + CHUNK, :], w_split, pair, r)
    for k in range(tiles.shape[0]):
        add_tile(coords, k, tiles[k], pair, acc)
    finish(acc, out)


def loading_kernel(
    coords_far, state_far, tiles_far, weight_far, out, pair, acc, state, tiles, weight, coords, sems
):
    count = tiles.shape[0]
    chunks, step = VERT // CHUNK, count // PIECES
    first = [
        pltpu.make_async_copy(weight_far, weight, sems.at[0]),
        pltpu.make_async_copy(coords_far, coords, sems.at[1]),
    ]
    states = [
        pltpu.make_async_copy(state_far.at[pl.ds(i * CHUNK, CHUNK)], state.at[pl.ds(i * CHUNK, CHUNK)], sems.at[2 + i])
        for i in range(chunks)
    ]
    lists = [
        pltpu.make_async_copy(
            tiles_far.at[pl.ds(i * step, step)], tiles.at[pl.ds(i * step, step)], sems.at[2 + chunks + i]
        )
        for i in range(PIECES)
    ]
    for copy in first + states:
        copy.start()
    acc[...] = jnp.zeros_like(acc)
    first[0].wait()
    w_split = split(weight[...])
    for i in range(chunks):
        states[i].wait()
        if i % 2 == 0:
            for copy in lists[i // 2 :: chunks // 2]:
                copy.start()
        weigh_rows(state[i * CHUNK : (i + 1) * CHUNK, :], w_split, pair, i * CHUNK)
    first[1].wait()
    for i in range(PIECES):
        lists[i].wait()
        for k in range(i * step, (i + 1) * step):
            add_tile(coords, k, tiles[k], pair, acc)
    finish(acc, out)


CHUNK, PIECES = 256, 4
SCRATCH = [pltpu.VMEM((2, NBLK, 2 * TILE, FEAT), BF), pltpu.VMEM((NBLK + 1, TILE, FEAT), F32)]


def cost(flops, moved):
    return pl.CostEstimate(flops=flops, bytes_accessed=moved, transcendentals=0)


def call(kernel, name, out_shape, in_specs, scratch, flops, moved, *args, params=PARAMS):
    return pl.pallas_call(
        kernel,
        out_shape=out_shape,
        in_specs=in_specs,
        out_specs=jax.tree.map(lambda _: VSPEC, out_shape),
        scratch_shapes=scratch,
        compiler_params=params,
        cost_estimate=cost(flops, moved),
        name=name,
    )(*args)


def product(coords, state, tiles, weight):
    return call(
        product_kernel, "product", WHOLE, [SSPEC, VSPEC, VSPEC, VSPEC], SCRATCH,
        3_200_000_000, 6 << 20, coords, state, tiles, weight,
    )


def loading_product(coords, state, tiles, weight):
    near = [pltpu.VMEM(x.shape, F32) for x in (state, tiles, weight)] + [pltpu.SMEM(coords.shape, jnp.int32)]
    sems = [pltpu.SemaphoreType.DMA((2 + VERT // CHUNK + PIECES,))]
    return call(
        loading_kernel, "loading_product", WHOLE, [FAR, FAR, FAR, FAR], SCRATCH + near + sems,
        3_200_000_000, 6 << 20, coords, state, tiles, weight, params=MOST,
    )


def mix_kernel(mixer, part, out):
    t_hi, t_lo = split(mixer[...])
    lhs = jnp.concatenate([t_hi, t_lo, t_hi, t_lo], axis=1)
    for h in range(2):
        cols = slice(h * HALF, (h + 1) * HALF)
        for i in range(0, OWN, 2):
            hi, lo = split(jnp.concatenate([part[:, i, cols], part[:, i + 1, cols]], axis=1))
            mixed = jnp.tanh(dot(lhs, jnp.concatenate([hi, hi, lo, lo], axis=0)))
            out[:, i, cols] = mixed[:, :HALF]
            out[:, i + 1, cols] = mixed[:, HALF:]


def mix(mixer, part):
    return call(mix_kernel, "mix", WHOLE, [VSPEC] * 2, [], 1_600_000_000, 4 << 20, mixer, part)


def exchange(x):
    return lax.all_to_all(x, "snap", split_axis=0, concat_axis=0, tiled=True)


def shards(features, tiles, coords, temporal, weight_one, weight_two):
    tiles = tiles.reshape(tiles.shape[1:])
    coords = coords[0].T
    mine = loading_product(coords, features.reshape(VERT, FEAT), tiles, weight_one)
    state = exchange(mix(temporal, exchange(mine)))
    mine = product(coords, state.reshape(VERT, FEAT), tiles, weight_two)
    return exchange(mix(temporal, exchange(mine))).reshape(features.shape)


def solution(mesh):
    return jax.shard_map(
        shards,
        mesh=mesh,
        in_specs=(
            P("snap", "rep", None),
            P("snap", "rep", None, None),
            P("snap", "rep", None),
            P(),
            P(),
            P(),
        ),
        out_specs=P("snap", "rep", None),
        check_vma=False,
    )
```

```python
import jax
import jax.numpy as jnp
import numpy as np
from jax import lax
from jax.experimental import pallas as pl
from jax.experimental.pallas import tpu as pltpu
from jax.sharding import PartitionSpec as P

NZ, NY, NC = 8, 4, 2
NYC = NY * NC
SNAPS = NZ * NYC
VERT, FEAT, TILE = 2048, 256, 128
HALF = FEAT // 2
OWN = VERT // SNAPS
PLANE = NZ * OWN
NBLK = VERT // TILE
BF, F32 = jnp.bfloat16, jnp.float32
LIST = [jax.ShapeDtypeStruct((NZ, OWN, HALF), F32)] * NYC
GRID = jax.ShapeDtypeStruct((NZ, NYC, OWN, HALF), F32)
FLAT = jax.ShapeDtypeStruct((VERT, HALF), F32)
PARAMS = pltpu.CompilerParams(vmem_limit_bytes=32 << 20)
MOST = pltpu.CompilerParams(vmem_limit_bytes=60 << 20)
VSPEC = pl.BlockSpec(memory_space=pltpu.VMEM)
SSPEC = pl.BlockSpec(memory_space=pltpu.SMEM)
FAR = pl.BlockSpec(memory_space=pl.ANY)


def split(x):
    hi = x.astype(BF)
    return hi, (x - hi.astype(F32)).astype(BF)


def dot(a, b):
    return jnp.dot(a, b, preferred_element_type=F32)


def put_block(pair, blk, value):
    hi, lo = split(value)
    both = jnp.concatenate([hi, lo], axis=1)
    pair[blk, :TILE] = both
    pair[blk, TILE:] = both


def add_tiles(coords, tiles, pair, acc, which):
    for k in which:
        row = coords[0, k]
        used = row >= 0
        row = jnp.where(used, row, NBLK)
        col = jnp.where(used, coords[1, k], 0)
        wide = dot(jnp.concatenate(split(tiles[k]), axis=1), pair[col])
        acc[row] += wide[:, :HALF] + wide[:, HALF:]


def tile_products(coords, tiles, pair, acc):
    acc[...] = jnp.zeros_like(acc)
    add_tiles(coords, tiles, pair, acc, range(tiles.shape[0]))


SCRATCH = [pltpu.VMEM((NBLK, 2 * TILE, FEAT), BF), pltpu.VMEM((NBLK + 1, TILE, HALF), F32)]


def cost(flops, moved):
    return pl.CostEstimate(flops=flops, bytes_accessed=moved, transcendentals=0)


def call(kernel, name, out_shape, in_specs, scratch, flops, moved, *args, params=PARAMS):
    return pl.pallas_call(
        kernel,
        out_shape=out_shape,
        in_specs=in_specs,
        out_specs=jax.tree.map(lambda _: VSPEC, out_shape),
        scratch_shapes=scratch,
        compiler_params=params,
        cost_estimate=cost(flops, moved),
        name=name,
    )(*args)


def column(pos, k, sign):
    y = lax.rem(pos[0] + NY + sign * (k // NC), NY)
    m = k % NC
    return y * NC + (1 - pos[1] if m else pos[1])


def planes(pos, acc):
    for k in range(NYC):
        a = column(pos, k, 1)
        yield k, acc[2 * a].reshape(NZ // 2, OWN, HALF), acc[2 * a + 1].reshape(NZ // 2, OWN, HALF)


def emit_list(pos, acc, outs):
    for k, low, high in planes(pos, acc):
        outs[k][: NZ // 2] = low
        outs[k][NZ // 2 :] = high


def emit_grid(pos, acc, out):
    for k, low, high in planes(pos, acc):
        out[: NZ // 2, k] = low
        out[NZ // 2 :, k] = high


def put_plane(pair, z, value):
    flat = value.reshape(PLANE, HALF)
    put_block(pair, 2 * z, flat[:TILE])
    put_block(pair, 2 * z + 1, flat[TILE:])


def weigh_state(state, weight, pair):
    w_hi, w_lo = split(weight[...])
    for r in range(0, VERT, PLANE):
        s_hi, s_lo = split(state[r : r + PLANE, :])
        u = dot(s_hi, w_hi) + (dot(s_hi, w_lo) + dot(s_lo, w_hi))
        put_block(pair, r // TILE, u[:TILE])
        put_block(pair, r // TILE + 1, u[TILE:])


def first_list_kernel(pos, coords, state, tiles, weight, *rest):
    outs, (pair, acc) = rest[:NZ], rest[NZ:]
    weigh_state(state, weight, pair)
    tile_products(coords, tiles, pair, acc)
    emit_list(pos, acc, outs)


def weigh_rows(rows, w_split, pair, blk):
    w_hi, w_lo = w_split
    s_hi, s_lo = split(rows)
    u = dot(s_hi, w_hi) + (dot(s_hi, w_lo) + dot(s_lo, w_hi))
    put_block(pair, blk, u[:TILE])
    put_block(pair, blk + 1, u[TILE:])


def first_grid_kernel(
    pos, coords_far, state_far, tiles_far, weight_far, out, pair, acc, state, tiles, weight, coords, sems
):
    chunks, step = VERT // PLANE, tiles.shape[0] // PIECES
    first = [
        pltpu.make_async_copy(weight_far.at[:, pl.ds(0, HALF)], weight, sems.at[0]),
        pltpu.make_async_copy(coords_far, coords, sems.at[1]),
    ]
    states = [
        pltpu.make_async_copy(state_far.at[pl.ds(i * PLANE, PLANE)], state.at[pl.ds(i * PLANE, PLANE)], sems.at[2 + i])
        for i in range(chunks)
    ]
    lists = [
        pltpu.make_async_copy(
            tiles_far.at[pl.ds(i * step, step)], tiles.at[pl.ds(i * step, step)], sems.at[2 + chunks + i]
        )
        for i in range(PIECES)
    ]
    for copy in first + states:
        copy.start()
    first[0].wait()
    w_split = split(weight[...])
    for i in range(chunks):
        states[i].wait()
        if i % 2 == 0:
            lists[i // 2].start()
        weigh_rows(state[i * PLANE : (i + 1) * PLANE, :], w_split, pair, 2 * i)
    first[1].wait()
    acc[...] = jnp.zeros_like(acc)
    for i in range(PIECES):
        lists[i].wait()
        add_tiles(coords, tiles, pair, acc, range(i * step, (i + 1) * step))
    emit_grid(pos, acc, out)


PIECES = 4


def first_list(*args):
    specs = [SSPEC, SSPEC, VSPEC, VSPEC, VSPEC]
    return call(first_list_kernel, "first_list", LIST, specs, SCRATCH, 1_600_000_000, 5 << 20, *args)


def first_grid(pos, coords, state, tiles, weight):
    near = [pltpu.VMEM(state.shape, F32), pltpu.VMEM(tiles.shape, F32), pltpu.VMEM((FEAT, HALF), F32)]
    near += [pltpu.SMEM(coords.shape, jnp.int32), pltpu.SemaphoreType.DMA((2 + VERT // PLANE + PIECES,))]
    return call(
        first_grid_kernel, "first_grid", GRID, [SSPEC] + [FAR] * 4, SCRATCH + near,
        1_600_000_000, 5 << 20, pos, coords, state, tiles, weight, params=MOST,
    )


def early_kernel(pos, coords, tiles, *rest):
    parts, (out, pair, acc) = rest[:NYC], rest[NYC:]
    for k in range(NYC):
        put_plane(pair, column(pos, k, -1), parts[k][...])
    tile_products(coords, tiles, pair, acc)
    out[...] = acc[:NBLK].reshape(VERT, HALF)


def early_product(pos, coords, tiles, parts):
    specs = [SSPEC, SSPEC] + [VSPEC] * (1 + NYC)
    return call(early_kernel, "early_product", FLAT, specs, SCRATCH, 800_000_000, 4 << 20, pos, coords, tiles, *parts)


def project(left, right, weight, acc):
    w_hi, w_lo = split(weight[...])
    for r in range(0, VERT, PLANE):
        x = jnp.concatenate([left[r : r + PLANE, :], right[r : r + PLANE, :]], axis=1)
        x_hi, x_lo = split(x)
        u = dot(x_hi, w_hi) + (dot(x_hi, w_lo) + dot(x_lo, w_hi))
        acc[r // TILE] = u[:TILE]
        acc[r // TILE + 1] = u[TILE:]


def late_kernel(pos, coords, tiles, left, weight, part, right, out, pair, acc):
    for k in range(NYC):
        put_plane(pair, column(pos, k, -1), part[:, k])
    tile_products(coords, tiles, pair, acc)
    right[...] = acc[:NBLK].reshape(VERT, HALF)
    project(left, right, weight, acc)
    emit_grid(pos, acc, out)


def late_product(*args):
    specs = [SSPEC, SSPEC] + [VSPEC] * 4
    return call(late_kernel, "late_product", [FLAT, GRID], specs, SCRATCH, 1_600_000_000, 6 << 20, *args)


def last_kernel(pos, left, right, weight, *rest):
    outs, (acc,) = rest[:NYC], rest[NYC:]
    project(left, right, weight, acc)
    emit_list(pos, acc, outs)


def last_project(*args):
    specs = [SSPEC] + [VSPEC] * 3
    return call(last_kernel, "last_project", LIST, specs, SCRATCH[1:], 800_000_000, 3 << 20, *args)


def mix_rows(mixer, load, store):
    t_hi, t_lo = split(mixer[...])
    lhs = jnp.concatenate([t_hi, t_lo, t_hi, t_lo], axis=1)
    for i in range(0, OWN, 2):
        hi, lo = split(jnp.concatenate([load(i), load(i + 1)], axis=1))
        h = jnp.tanh(dot(lhs, jnp.concatenate([hi, hi, lo, lo], axis=0)))
        store(i, h[:, :HALF])
        store(i + 1, h[:, HALF:])


def mix_to_list_kernel(mixer, part, *outs):
    def load(i):
        return jnp.concatenate([part[a, :, i, :] for a in range(NYC)], axis=0)

    def store(i, h):
        for k in range(NZ):
            outs[k][:, i, :] = h[NYC * k : NYC * k + NYC]

    mix_rows(mixer, load, store)


def mix_to_grid_kernel(mixer, *refs):
    parts, out = refs[:NZ], refs[NZ]

    def load(i):
        return jnp.concatenate([p[:, i, :] for p in parts], axis=0)

    def store(i, h):
        for a in range(NYC):
            out[a, :, i, :] = h[NZ * a : NZ * a + NZ]

    mix_rows(mixer, load, store)


def mix_to_list(mixer, part):
    return call(mix_to_list_kernel, "mix_to_list", LIST, [VSPEC] * 2, [], 800_000_000, 2 << 20, mixer, part)


def mix_to_grid(mixer, parts):
    return call(
        mix_to_grid_kernel, "mix_to_grid", GRID, [VSPEC] * (1 + NZ), [], 800_000_000, 2 << 20, mixer, *parts
    )


def join_kernel(*refs):
    for k in range(NZ):
        refs[NZ][:, k] = refs[k][...]


def join(parts):
    return call(join_kernel, "join", GRID, [VSPEC] * NZ, [], 0, 2 << 20, *parts)


def part_kernel(part, *outs):
    for k in range(NZ):
        outs[k][...] = part[:, k]


def separate(part):
    return call(part_kernel, "separate", LIST, [VSPEC], [], 0, 2 << 20, part)


def assemble_kernel(pos, right, *refs):
    left, out = refs[:NYC], refs[NYC]
    for k in range(NYC):
        rows = pl.ds(pl.multiple_of(column(pos, k, -1) * PLANE, PLANE), PLANE)
        out[rows, :HALF] = left[k][...].reshape(PLANE, HALF)
        out[rows, HALF:] = right[:, k].reshape(PLANE, HALF)


def assemble(pos, left, right):
    shape = jax.ShapeDtypeStruct((VERT, FEAT), F32)
    return call(assemble_kernel, "assemble", shape, [SSPEC] + [VSPEC] * (1 + NYC), [], 0, 4 << 20, pos, right, *left)


RING = (0, 4, 1, 5, 2, 6, 3, 7)
GROUPS = [[z * NYC + a for z in RING] for a in range(NYC)]


def along_z(x):
    return lax.all_to_all(x, "snap", 0, 0, tiled=True, axis_index_groups=GROUPS)


def along_y(parts):
    got = [parts[0]] * NYC
    for k in (4, 5, 2, 6, 3, 7, 1):
        pairs = []
        for s in range(SNAPS):
            z, y, c = s // NYC, s // NC % NY, s % NC
            pairs.append((s, (z * NY + (y + k // NC) % NY) * NC + (c + k) % NC))
        got[k] = lax.ppermute(parts[k], "snap", pairs)
    return got


def shards(features, tiles, coords, temporal, weight_one, weight_two):
    me = lax.axis_index("snap")
    y, c = me // NC % NY, me % NC
    pos = jnp.stack([y, c]).astype(jnp.int32)
    state = features.reshape(VERT, FEAT)
    tiles = tiles.reshape(tiles.shape[1:])
    coords = coords[0].T

    def places(sign, list_major):
        ids = np.arange(SNAPS)
        k, a = (ids // NZ, ids % NZ) if list_major else (ids % NYC, ids // NYC)
        plane = jnp.asarray(np.array(RING)[a] * NYC, jnp.int32)
        step = jnp.asarray(sign * (k // NC) + NY, jnp.int32)
        return plane + (y + step) % NY * NC + (c + jnp.asarray(k, jnp.int32)) % NC

    ids = jnp.arange(SNAPS, dtype=jnp.int32)

    def mixer(rows, cols):
        left = (rows[:, None] == ids[None, :]).astype(F32)
        right = (cols[None, :] == ids[:, None]).astype(F32)
        high = lax.Precision.HIGHEST
        return jnp.dot(jnp.dot(left, temporal, precision=high), right, precision=high)

    mix_b = mixer(places(1, True), places(-1, False))
    mix_a = mixer(places(1, False), places(-1, True))

    a = first_grid(pos, coords, state, tiles, weight_one)
    b = first_list(pos, coords, state, tiles, weight_one[:, HALF:])
    for depth in range(2):
        a = along_y(separate(along_z(a)))
        b = along_z(join(along_y(b)))
        a = mix_to_grid(mix_a, a)
        b = mix_to_list(mix_b, b)
        a = along_y(separate(along_z(a)))
        b = along_z(join(along_y(b)))
        if depth == 0:
            left = early_product(pos, coords, tiles, a)
            right, a = late_product(pos, coords, tiles, left, weight_two[:, :HALF], b)
            b = last_project(pos, left, right, weight_two[:, HALF:])
    return assemble(pos, a, b).reshape(features.shape)


def solution(mesh):
    return jax.shard_map(
        shards,
        mesh=mesh,
        in_specs=(
            P("snap", "rep", None),
            P("snap", "rep", None, None),
            P("snap", "rep", None),
            P(),
            P(),
            P(),
        ),
        out_specs=P("snap", "rep", None),
        check_vma=False,
    )
```

```python
import jax
import jax.numpy as jnp
from jax import lax
from jax.experimental import pallas as pl
from jax.experimental.pallas import tpu as pltpu
from jax.sharding import PartitionSpec as P

SNAPS = 64
VERT, FEAT, TILE = 2048, 256, 128
HALF = FEAT // 2
OWN = VERT // SNAPS
NBLK = VERT // TILE
BF, F32 = jnp.bfloat16, jnp.float32
WHOLE = jax.ShapeDtypeStruct((SNAPS, OWN, FEAT), F32)
PARAMS = pltpu.CompilerParams(vmem_limit_bytes=32 << 20)
MOST = pltpu.CompilerParams(vmem_limit_bytes=60 << 20)
VSPEC = pl.BlockSpec(memory_space=pltpu.VMEM)
SSPEC = pl.BlockSpec(memory_space=pltpu.SMEM)
FAR = pl.BlockSpec(memory_space=pl.ANY)


def split(x):
    hi = x.astype(BF)
    return hi, (x - hi.astype(F32)).astype(BF)


def dot(a, b):
    return jnp.dot(a, b, preferred_element_type=F32)


def put_block(pair, h, blk, value):
    hi, lo = split(value)
    both = jnp.concatenate([hi, lo], axis=1)
    pair[h, blk, :TILE] = both
    pair[h, blk, TILE:] = both


def weigh_rows(rows, w_split, pair, r):
    w_hi, w_lo = w_split
    s_hi, s_lo = split(rows)
    u = dot(s_hi, w_hi) + (dot(s_hi, w_lo) + dot(s_lo, w_hi))
    for q in range(0, rows.shape[0], TILE):
        for h in range(2):
            put_block(pair, h, (r + q) // TILE, u[q : q + TILE, h * HALF : (h + 1) * HALF])


def add_tile(coords, k, tile, pair, acc):
    row = coords[0, k]
    used = row >= 0
    row = jnp.where(used, row, NBLK)
    col = jnp.where(used, coords[1, k], 0)
    lhs = jnp.concatenate(split(tile), axis=1)
    for h in range(2):
        wide = dot(lhs, pair[h, col])
        acc[row, :, h * HALF : (h + 1) * HALF] += wide[:, :HALF] + wide[:, HALF:]


def finish(acc, out):
    out[...] = acc[:NBLK].reshape(SNAPS, OWN, FEAT)


def product_kernel(coords, state, tiles, weight, out, pair, acc):
    w_split = split(weight[...])
    acc[...] = jnp.zeros_like(acc)
    for r in range(0, VERT, CHUNK):
        weigh_rows(state[r : r + CHUNK, :], w_split, pair, r)
    for k in range(tiles.shape[0]):
        add_tile(coords, k, tiles[k], pair, acc)
    finish(acc, out)


def loading_kernel(
    coords_far, state_far, tiles_far, weight_far, out_far, pair, acc, state, tiles, weight, coords, sems
):
    count = tiles.shape[0]
    chunks, step = VERT // CHUNK, count // PIECES
    first = [
        pltpu.make_async_copy(weight_far, weight, sems.at[0]),
        pltpu.make_async_copy(coords_far, coords, sems.at[1]),
    ]
    states = [
        pltpu.make_async_copy(state_far.at[pl.ds(i * CHUNK, CHUNK)], state.at[pl.ds(i * CHUNK, CHUNK)], sems.at[2 + i])
        for i in range(chunks)
    ]
    lists = [
        pltpu.make_async_copy(
            tiles_far.at[pl.ds(i * step, step)], tiles.at[pl.ds(i * step, step)], sems.at[2 + chunks + i]
        )
        for i in range(PIECES)
    ]
    sends = [
        pltpu.make_async_copy(
            state.at[pl.ds(i * CHUNK, CHUNK)], out_far.at[pl.ds(i * CHUNK, CHUNK)], sems.at[2 + chunks + PIECES + i]
        )
        for i in range(chunks)
    ]
    for copy in first + states + lists:
        copy.start()
    acc[...] = jnp.zeros_like(acc)
    for i in range(chunks):
        states[i].wait()
        for blk in range(i * CHUNK // TILE, (i + 1) * CHUNK // TILE):
            for h in range(2):
                put_block(pair, h, blk, state[blk * TILE : (blk + 1) * TILE, h * HALF : (h + 1) * HALF])
    first[1].wait()
    for i in range(PIECES):
        lists[i].wait()
        for k in range(i * step, (i + 1) * step):
            add_tile(coords, k, tiles[k], pair, acc)
    first[0].wait()
    w_hi, w_lo = split(weight[...])
    for i in range(chunks):
        blks = slice(i * CHUNK // TILE, (i + 1) * CHUNK // TILE)
        s_hi, s_lo = split(acc[blks].reshape(CHUNK, FEAT))
        state[i * CHUNK : (i + 1) * CHUNK, :] = dot(s_hi, w_hi) + (dot(s_hi, w_lo) + dot(s_lo, w_hi))
        sends[i].start()
    for copy in sends:
        copy.wait()


CHUNK, PIECES = 256, 4
SCRATCH = [pltpu.VMEM((2, NBLK, 2 * TILE, FEAT), BF), pltpu.VMEM((NBLK + 1, TILE, FEAT), F32)]


def cost(flops, moved):
    return pl.CostEstimate(flops=flops, bytes_accessed=moved, transcendentals=0)


def call(kernel, name, out_shape, in_specs, scratch, flops, moved, *args, params=PARAMS, out_spec=VSPEC):
    return pl.pallas_call(
        kernel,
        out_shape=out_shape,
        in_specs=in_specs,
        out_specs=out_spec,
        scratch_shapes=scratch,
        compiler_params=params,
        cost_estimate=cost(flops, moved),
        name=name,
    )(*args)


def product(coords, state, tiles, weight):
    return call(
        product_kernel, "product", WHOLE, [SSPEC, VSPEC, VSPEC, VSPEC], SCRATCH,
        3_200_000_000, 6 << 20, coords, state, tiles, weight,
    )


def loading_product(coords, state, tiles, weight):
    near = [pltpu.VMEM(x.shape, F32) for x in (state, tiles, weight)] + [pltpu.SMEM(coords.shape, jnp.int32)]
    sems = [pltpu.SemaphoreType.DMA((2 + 2 * VERT // CHUNK + PIECES,))]
    out = jax.ShapeDtypeStruct((VERT, FEAT), F32)
    mine = call(
        loading_kernel, "loading_product", out, [FAR] * 4, SCRATCH + near + sems,
        3_200_000_000, 6 << 20, coords, state, tiles, weight, params=MOST, out_spec=FAR,
    )
    return mine.reshape(WHOLE.shape)


def mix_kernel(mixer, part, out):
    t_hi, t_lo = split(mixer[...])
    lhs = jnp.concatenate([t_hi, t_lo, t_hi, t_lo], axis=1)
    for h in range(2):
        cols = slice(h * HALF, (h + 1) * HALF)
        for i in range(0, OWN, 2):
            hi, lo = split(jnp.concatenate([part[:, i, cols], part[:, i + 1, cols]], axis=1))
            mixed = jnp.tanh(dot(lhs, jnp.concatenate([hi, hi, lo, lo], axis=0)))
            out[:, i, cols] = mixed[:, :HALF]
            out[:, i + 1, cols] = mixed[:, HALF:]


def mix(mixer, part):
    return call(mix_kernel, "mix", WHOLE, [VSPEC] * 2, [], 1_600_000_000, 4 << 20, mixer, part)


def exchange(x):
    return lax.all_to_all(x, "snap", split_axis=0, concat_axis=0, tiled=True)


def shards(features, tiles, coords, temporal, weight_one, weight_two):
    tiles = tiles.reshape(tiles.shape[1:])
    coords = coords[0].T
    mine = loading_product(coords, features.reshape(VERT, FEAT), tiles, weight_one)
    state = exchange(mix(temporal, exchange(mine)))
    mine = product(coords, state.reshape(VERT, FEAT), tiles, weight_two)
    return exchange(mix(temporal, exchange(mine))).reshape(features.shape)


def solution(mesh):
    return jax.shard_map(
        shards,
        mesh=mesh,
        in_specs=(
            P("snap", "rep", None),
            P("snap", "rep", None, None),
            P("snap", "rep", None),
            P(),
            P(),
            P(),
        ),
        out_specs=P("snap", "rep", None),
        check_vma=False,
    )
```

```python
import jax
import jax.numpy as jnp
from jax import lax
from jax.experimental import pallas as pl
from jax.experimental.pallas import tpu as pltpu
from jax.sharding import PartitionSpec as P

SNAPS = 64
VERT, FEAT, TILE = 2048, 256, 128
HALF = FEAT // 2
OWN = VERT // SNAPS
NBLK = VERT // TILE
BF, F32 = jnp.bfloat16, jnp.float32
WHOLE = jax.ShapeDtypeStruct((SNAPS, OWN, FEAT), F32)
PARAMS = pltpu.CompilerParams(vmem_limit_bytes=32 << 20)
MOST = pltpu.CompilerParams(vmem_limit_bytes=60 << 20)
VSPEC = pl.BlockSpec(memory_space=pltpu.VMEM)
SSPEC = pl.BlockSpec(memory_space=pltpu.SMEM)
FAR = pl.BlockSpec(memory_space=pl.ANY)


def split(x):
    hi = x.astype(BF)
    return hi, (x - hi.astype(F32)).astype(BF)


def dot(a, b):
    return jnp.dot(a, b, preferred_element_type=F32)


def put_block(pair, h, blk, value):
    hi, lo = split(value)
    both = jnp.concatenate([hi, lo], axis=1)
    pair[h, blk, :TILE] = both
    pair[h, blk, TILE:] = both


def weigh_rows(rows, w_split, pair, r):
    w_hi, w_lo = w_split
    s_hi, s_lo = split(rows)
    u = dot(s_hi, w_hi) + (dot(s_hi, w_lo) + dot(s_lo, w_hi))
    for q in range(0, rows.shape[0], TILE):
        for h in range(2):
            put_block(pair, h, (r + q) // TILE, u[q : q + TILE, h * HALF : (h + 1) * HALF])


def add_tile(coords, k, tile, pair, acc):
    row = coords[0, k]
    used = row >= 0
    row = jnp.where(used, row, NBLK)
    col = jnp.where(used, coords[1, k], 0)
    lhs = jnp.concatenate(split(tile), axis=1)
    for h in range(2):
        wide = dot(lhs, pair[h, col])
        acc[row, :, h * HALF : (h + 1) * HALF] += wide[:, :HALF] + wide[:, HALF:]


def finish(acc, out):
    out[...] = acc[:NBLK].reshape(SNAPS, OWN, FEAT)


def product_kernel(coords, state, tiles, weight, out, pair, acc):
    w_split = split(weight[...])
    acc[...] = jnp.zeros_like(acc)
    for r in range(0, VERT, CHUNK):
        weigh_rows(state[r : r + CHUNK, :], w_split, pair, r)
    for k in range(tiles.shape[0]):
        add_tile(coords, k, tiles[k], pair, acc)
    finish(acc, out)


def loading_kernel(
    coords_far, state_far, tiles_far, weight_far, out_far, pair, acc, state, tiles, weight, coords, sems
):
    count = tiles.shape[0]
    chunks, step = VERT // CHUNK, count // PIECES
    first = [
        pltpu.make_async_copy(weight_far, weight, sems.at[0]),
        pltpu.make_async_copy(coords_far, coords, sems.at[1]),
    ]
    states = [
        pltpu.make_async_copy(state_far.at[pl.ds(i * CHUNK, CHUNK)], state.at[pl.ds(i * CHUNK, CHUNK)], sems.at[2 + i])
        for i in range(chunks)
    ]
    lists = [
        pltpu.make_async_copy(
            tiles_far.at[pl.ds(i * step, step)], tiles.at[pl.ds(i * step, step)], sems.at[2 + chunks + i]
        )
        for i in range(PIECES)
    ]
    sends = [
        pltpu.make_async_copy(
            state.at[pl.ds(i * CHUNK, CHUNK)], out_far.at[pl.ds(i * CHUNK, CHUNK)], sems.at[2 + chunks + PIECES + i]
        )
        for i in range(chunks)
    ]
    for copy in first + states + lists:
        copy.start()
    acc[...] = jnp.zeros_like(acc)
    for i in range(chunks):
        states[i].wait()
        for blk in range(i * CHUNK // TILE, (i + 1) * CHUNK // TILE):
            for h in range(2):
                put_block(pair, h, blk, state[blk * TILE : (blk + 1) * TILE, h * HALF : (h + 1) * HALF])
    first[1].wait()
    for i in range(PIECES):
        lists[i].wait()
        for k in range(i * step, (i + 1) * step):
            add_tile(coords, k, tiles[k], pair, acc)
    first[0].wait()
    w_hi, w_lo = split(weight[...])
    for i in range(chunks):
        blks = slice(i * CHUNK // TILE, (i + 1) * CHUNK // TILE)
        s_hi, s_lo = split(acc[blks].reshape(CHUNK, FEAT))
        state[i * CHUNK : (i + 1) * CHUNK, :] = dot(s_hi, w_hi) + (dot(s_hi, w_lo) + dot(s_lo, w_hi))
        sends[i].start()
    for copy in sends:
        copy.wait()


CHUNK, PIECES = 256, 4
SCRATCH = [pltpu.VMEM((2, NBLK, 2 * TILE, FEAT), BF), pltpu.VMEM((NBLK + 1, TILE, FEAT), F32)]


def cost(flops, moved):
    return pl.CostEstimate(flops=flops, bytes_accessed=moved, transcendentals=0)


def call(kernel, name, out_shape, in_specs, scratch, flops, moved, *args, params=PARAMS, out_spec=VSPEC):
    return pl.pallas_call(
        kernel,
        out_shape=out_shape,
        in_specs=in_specs,
        out_specs=out_spec,
        scratch_shapes=scratch,
        compiler_params=params,
        cost_estimate=cost(flops, moved),
        name=name,
    )(*args)


def product(coords, state, tiles, weight):
    return call(
        product_kernel, "product", WHOLE, [SSPEC, VSPEC, VSPEC, VSPEC], SCRATCH,
        3_200_000_000, 6 << 20, coords, state, tiles, weight,
    )


def loading_product(coords, state, tiles, weight):
    near = [pltpu.VMEM(x.shape, F32) for x in (state, tiles, weight)] + [pltpu.SMEM(coords.shape, jnp.int32)]
    sems = [pltpu.SemaphoreType.DMA((2 + 2 * VERT // CHUNK + PIECES,))]
    out = jax.ShapeDtypeStruct((VERT, FEAT), F32)
    mine = call(
        loading_kernel, "loading_product", out, [FAR] * 4, SCRATCH + near + sems,
        3_200_000_000, 6 << 20, coords, state, tiles, weight, params=MOST, out_spec=FAR,
    )
    return mine.reshape(WHOLE.shape)


def mix_kernel(mixer, part, out):
    t_hi, t_lo = split(mixer[...])
    lhs = jnp.concatenate([t_hi, t_lo, t_hi, t_lo], axis=1)
    for g in range(0, OWN, 8):
        rows = slice(g, g + 8)
        x = jnp.swapaxes(part[:, rows, :], 0, 1)
        mixed = []
        for i in range(8):
            hi, lo = split(x[i])
            mixed.append(jnp.tanh(dot(lhs, jnp.concatenate([hi, hi, lo, lo], axis=0))))
        out[:, rows, :] = jnp.swapaxes(jnp.stack(mixed), 0, 1)


def mix(mixer, part):
    return call(mix_kernel, "mix", WHOLE, [VSPEC] * 2, [], 1_600_000_000, 4 << 20, mixer, part)


def exchange(x):
    return lax.all_to_all(x, "snap", split_axis=0, concat_axis=0, tiled=True)


def shards(features, tiles, coords, temporal, weight_one, weight_two):
    tiles = tiles.reshape(tiles.shape[1:])
    coords = coords[0].T
    mine = loading_product(coords, features.reshape(VERT, FEAT), tiles, weight_one)
    state = exchange(mix(temporal, exchange(mine)))
    mine = product(coords, state.reshape(VERT, FEAT), tiles, weight_two)
    return exchange(mix(temporal, exchange(mine))).reshape(features.shape)


def solution(mesh):
    return jax.shard_map(
        shards,
        mesh=mesh,
        in_specs=(
            P("snap", "rep", None),
            P("snap", "rep", None, None),
            P("snap", "rep", None),
            P(),
            P(),
            P(),
        ),
        out_specs=P("snap", "rep", None),
        check_vma=False,
    )
```

```python
import jax
import jax.numpy as jnp
from jax import lax
from jax.experimental import pallas as pl
from jax.experimental.pallas import tpu as pltpu
from jax.sharding import PartitionSpec as P

SNAPS = 64
VERT, FEAT, TILE = 2048, 256, 128
HALF = FEAT // 2
OWN = VERT // SNAPS
NBLK = VERT // TILE
BF, F32 = jnp.bfloat16, jnp.float32
WHOLE = jax.ShapeDtypeStruct((SNAPS, OWN, FEAT), F32)
PARAMS = pltpu.CompilerParams(vmem_limit_bytes=32 << 20)
MOST = pltpu.CompilerParams(vmem_limit_bytes=60 << 20)
VSPEC = pl.BlockSpec(memory_space=pltpu.VMEM)
SSPEC = pl.BlockSpec(memory_space=pltpu.SMEM)
FAR = pl.BlockSpec(memory_space=pl.ANY)


def split(x):
    hi = x.astype(BF)
    return hi, (x - hi.astype(F32)).astype(BF)


def dot(a, b):
    return jnp.dot(a, b, preferred_element_type=F32)


def put_block(pair, h, blk, value):
    hi, lo = split(value)
    both = jnp.concatenate([hi, lo], axis=1)
    pair[h, blk, :TILE] = both
    pair[h, blk, TILE:] = both


def add_tile(coords, k, tile, pair, acc):
    row = coords[0, k]
    used = row >= 0
    row = jnp.where(used, row, NBLK)
    col = jnp.where(used, coords[1, k], 0)
    lhs = jnp.concatenate(split(tile), axis=1)
    for h in range(2):
        wide = dot(lhs, pair[h, col])
        acc[row, :, h * HALF : (h + 1) * HALF] += wide[:, :HALF] + wide[:, HALF:]


def finish(acc, out):
    out[...] = acc[:NBLK].reshape(SNAPS, OWN, FEAT)


def put_state(state, pair, blk):
    for h in range(2):
        put_block(pair, h, blk, state[blk * TILE : (blk + 1) * TILE, h * HALF : (h + 1) * HALF])


def weigh(rows, w_split):
    w_hi, w_lo = w_split
    s_hi, s_lo = split(rows)
    return dot(s_hi, w_hi) + (dot(s_hi, w_lo) + dot(s_lo, w_hi))


def sum_kernel(coords, state, tiles, out, pair, acc):
    acc[...] = jnp.zeros_like(acc)
    for blk in range(NBLK):
        put_state(state, pair, blk)
    for k in range(tiles.shape[0]):
        add_tile(coords, k, tiles[k], pair, acc)
    finish(acc, out)


def loading_kernel(
    coords_far, state_far, tiles_far, weight_far, out_far, pair, acc, state, tiles, weight, coords, sems
):
    count = tiles.shape[0]
    chunks, step = VERT // CHUNK, count // PIECES
    first = [
        pltpu.make_async_copy(weight_far, weight, sems.at[0]),
        pltpu.make_async_copy(coords_far, coords, sems.at[1]),
    ]
    states = [
        pltpu.make_async_copy(state_far.at[pl.ds(i * CHUNK, CHUNK)], state.at[pl.ds(i * CHUNK, CHUNK)], sems.at[2 + i])
        for i in range(chunks)
    ]
    lists = [
        pltpu.make_async_copy(
            tiles_far.at[pl.ds(i * step, step)], tiles.at[pl.ds(i * step, step)], sems.at[2 + chunks + i]
        )
        for i in range(PIECES)
    ]
    sends = [
        pltpu.make_async_copy(
            state.at[pl.ds(i * CHUNK, CHUNK)], out_far.at[pl.ds(i * CHUNK, CHUNK)], sems.at[2 + chunks + PIECES + i]
        )
        for i in range(chunks)
    ]
    for copy in first + states + lists:
        copy.start()
    acc[...] = jnp.zeros_like(acc)
    for i in range(chunks):
        states[i].wait()
        for blk in range(i * CHUNK // TILE, (i + 1) * CHUNK // TILE):
            put_state(state, pair, blk)
    first[1].wait()
    for i in range(PIECES):
        lists[i].wait()
        for k in range(i * step, (i + 1) * step):
            add_tile(coords, k, tiles[k], pair, acc)
    first[0].wait()
    w_split = split(weight[...])
    for i in range(chunks):
        blks = slice(i * CHUNK // TILE, (i + 1) * CHUNK // TILE)
        state[i * CHUNK : (i + 1) * CHUNK, :] = weigh(acc[blks].reshape(CHUNK, FEAT), w_split)
        sends[i].start()
    for copy in sends:
        copy.wait()


CHUNK, PIECES = 256, 4
SCRATCH = [pltpu.VMEM((2, NBLK, 2 * TILE, FEAT), BF), pltpu.VMEM((NBLK + 1, TILE, FEAT), F32)]


def cost(flops, moved):
    return pl.CostEstimate(flops=flops, bytes_accessed=moved, transcendentals=0)


def call(kernel, name, out_shape, in_specs, scratch, flops, moved, *args, params=PARAMS, out_spec=VSPEC):
    return pl.pallas_call(
        kernel,
        out_shape=out_shape,
        in_specs=in_specs,
        out_specs=out_spec,
        scratch_shapes=scratch,
        compiler_params=params,
        cost_estimate=cost(flops, moved),
        name=name,
    )(*args)


def tile_sum(coords, state, tiles):
    return call(
        sum_kernel, "tile_sum", WHOLE, [SSPEC, VSPEC, VSPEC], SCRATCH,
        1_600_000_000, 6 << 20, coords, state, tiles,
    )


def loading_product(coords, state, tiles, weight):
    near = [pltpu.VMEM(x.shape, F32) for x in (state, tiles, weight)] + [pltpu.SMEM(coords.shape, jnp.int32)]
    sems = [pltpu.SemaphoreType.DMA((2 + 2 * VERT // CHUNK + PIECES,))]
    out = jax.ShapeDtypeStruct((VERT, FEAT), F32)
    mine = call(
        loading_kernel, "loading_product", out, [FAR] * 4, SCRATCH + near + sems,
        3_200_000_000, 6 << 20, coords, state, tiles, weight, params=MOST, out_spec=FAR,
    )
    return mine.reshape(WHOLE.shape)


def mixed_rows(mixer, part):
    t_hi, t_lo = split(mixer[...])
    lhs = jnp.concatenate([t_hi, t_lo, t_hi, t_lo], axis=1)
    for g in range(0, OWN, 8):
        rows = slice(g, g + 8)
        x = jnp.swapaxes(part[:, rows, :], 0, 1)
        mixed = []
        for i in range(8):
            hi, lo = split(x[i])
            mixed.append(jnp.tanh(dot(lhs, jnp.concatenate([hi, hi, lo, lo], axis=0))))
        yield rows, jnp.stack(mixed)


def mix_kernel(mixer, part, out):
    for rows, mixed in mixed_rows(mixer, part):
        out[:, rows, :] = jnp.swapaxes(mixed, 0, 1)


def mix_weigh_kernel(mixer, weight, part, out):
    w_split = split(weight[...])
    for rows, mixed in mixed_rows(mixer, part):
        done = weigh(mixed.reshape(8 * SNAPS, FEAT), w_split)
        out[:, rows, :] = jnp.swapaxes(done.reshape(8, SNAPS, FEAT), 0, 1)


def mix(mixer, part):
    return call(mix_kernel, "mix", WHOLE, [VSPEC] * 2, [], 1_600_000_000, 4 << 20, mixer, part)


def mix_weigh(mixer, weight, part):
    return call(
        mix_weigh_kernel, "mix_weigh", WHOLE, [VSPEC] * 3, [], 2_400_000_000, 4 << 20, mixer, weight, part
    )


def exchange(x):
    return lax.all_to_all(x, "snap", split_axis=0, concat_axis=0, tiled=True)


def shards(features, tiles, coords, temporal, weight_one, weight_two):
    tiles = tiles.reshape(tiles.shape[1:])
    coords = coords[0].T
    mine = loading_product(coords, features.reshape(VERT, FEAT), tiles, weight_one)
    state = exchange(mix_weigh(temporal, weight_two, exchange(mine)))
    mine = tile_sum(coords, state.reshape(VERT, FEAT), tiles)
    return exchange(mix(temporal, exchange(mine))).reshape(features.shape)


def solution(mesh):
    return jax.shard_map(
        shards,
        mesh=mesh,
        in_specs=(
            P("snap", "rep", None),
            P("snap", "rep", None, None),
            P("snap", "rep", None),
            P(),
            P(),
            P(),
        ),
        out_specs=P("snap", "rep", None),
        check_vma=False,
    )
```

```python
import jax
import jax.numpy as jnp
from jax import lax
from jax.experimental import pallas as pl
from jax.experimental.pallas import tpu as pltpu
from jax.sharding import PartitionSpec as P

SNAPS = 64
VERT, FEAT, TILE = 2048, 256, 128
HALF = FEAT // 2
OWN = VERT // SNAPS
NBLK = VERT // TILE
BF, F32 = jnp.bfloat16, jnp.float32
WHOLE = jax.ShapeDtypeStruct((SNAPS, OWN, FEAT), F32)
PARAMS = pltpu.CompilerParams(vmem_limit_bytes=32 << 20)
MOST = pltpu.CompilerParams(vmem_limit_bytes=60 << 20)
VSPEC = pl.BlockSpec(memory_space=pltpu.VMEM)
SSPEC = pl.BlockSpec(memory_space=pltpu.SMEM)
FAR = pl.BlockSpec(memory_space=pl.ANY)


def split(x):
    hi = x.astype(BF)
    return hi, (x - hi.astype(F32)).astype(BF)


def dot(a, b):
    return jnp.dot(a, b, preferred_element_type=F32)


def add_tile(coords, k, tile, pair, acc):
    row = coords[0, k]
    used = row >= 0
    row = jnp.where(used, row, NBLK)
    col = jnp.where(used, coords[1, k], 0)
    a_hi, a_lo = split(tile)
    high = pair[0, col]
    both = jnp.concatenate([high, pair[1, col]], axis=0)
    acc[row] += dot(jnp.concatenate([a_hi, a_hi], axis=1), both) + dot(a_lo, high)


def finish(acc, out):
    out[...] = acc[:NBLK].reshape(SNAPS, OWN, FEAT)


def put_state(state, pair, blk):
    pair[0, blk], pair[1, blk] = split(state[blk * TILE : (blk + 1) * TILE, :])


def weigh(rows, w_split):
    w_hi, w_lo = w_split
    s_hi, s_lo = split(rows)
    return dot(s_hi, w_hi) + (dot(s_hi, w_lo) + dot(s_lo, w_hi))


def sum_kernel(coords, state, tiles, out, pair, acc):
    acc[...] = jnp.zeros_like(acc)
    for blk in range(NBLK):
        put_state(state, pair, blk)
    for k in range(tiles.shape[0]):
        add_tile(coords, k, tiles[k], pair, acc)
    finish(acc, out)


def loading_kernel(
    coords_far, state_far, tiles_far, weight_far, out_far, pair, acc, state, tiles, weight, coords, sems
):
    count = tiles.shape[0]
    chunks, step = VERT // CHUNK, count // PIECES
    first = [
        pltpu.make_async_copy(weight_far, weight, sems.at[0]),
        pltpu.make_async_copy(coords_far, coords, sems.at[1]),
    ]
    states = [
        pltpu.make_async_copy(state_far.at[pl.ds(i * CHUNK, CHUNK)], state.at[pl.ds(i * CHUNK, CHUNK)], sems.at[2 + i])
        for i in range(chunks)
    ]
    lists = [
        pltpu.make_async_copy(
            tiles_far.at[pl.ds(i * step, step)], tiles.at[pl.ds(i * step, step)], sems.at[2 + chunks + i]
        )
        for i in range(PIECES)
    ]
    sends = [
        pltpu.make_async_copy(
            state.at[pl.ds(i * CHUNK, CHUNK)], out_far.at[pl.ds(i * CHUNK, CHUNK)], sems.at[2 + chunks + PIECES + i]
        )
        for i in range(chunks)
    ]
    for copy in first + states + lists:
        copy.start()
    acc[...] = jnp.zeros_like(acc)
    for i in range(chunks):
        states[i].wait()
        for blk in range(i * CHUNK // TILE, (i + 1) * CHUNK // TILE):
            put_state(state, pair, blk)
    first[1].wait()
    for i in range(PIECES):
        lists[i].wait()
        for k in range(i * step, (i + 1) * step):
            add_tile(coords, k, tiles[k], pair, acc)
    first[0].wait()
    w_split = split(weight[...])
    for i in range(chunks):
        blks = slice(i * CHUNK // TILE, (i + 1) * CHUNK // TILE)
        state[i * CHUNK : (i + 1) * CHUNK, :] = weigh(acc[blks].reshape(CHUNK, FEAT), w_split)
        sends[i].start()
    for copy in sends:
        copy.wait()


CHUNK, PIECES = 256, 8
SCRATCH = [pltpu.VMEM((2, NBLK, TILE, FEAT), BF), pltpu.VMEM((NBLK + 1, TILE, FEAT), F32)]


def cost(flops, moved):
    return pl.CostEstimate(flops=flops, bytes_accessed=moved, transcendentals=0)


def call(kernel, name, out_shape, in_specs, scratch, flops, moved, *args, params=PARAMS, out_spec=VSPEC):
    return pl.pallas_call(
        kernel,
        out_shape=out_shape,
        in_specs=in_specs,
        out_specs=out_spec,
        scratch_shapes=scratch,
        compiler_params=params,
        cost_estimate=cost(flops, moved),
        name=name,
    )(*args)


def tile_sum(coords, state, tiles):
    return call(
        sum_kernel, "tile_sum", WHOLE, [SSPEC, VSPEC, VSPEC], SCRATCH,
        1_600_000_000, 6 << 20, coords, state, tiles,
    )


def loading_product(coords, state, tiles, weight):
    near = [pltpu.VMEM(x.shape, F32) for x in (state, tiles, weight)] + [pltpu.SMEM(coords.shape, jnp.int32)]
    sems = [pltpu.SemaphoreType.DMA((2 + 2 * VERT // CHUNK + PIECES,))]
    out = jax.ShapeDtypeStruct((VERT, FEAT), F32)
    mine = call(
        loading_kernel, "loading_product", out, [FAR] * 4, SCRATCH + near + sems,
        3_200_000_000, 6 << 20, coords, state, tiles, weight, params=MOST, out_spec=FAR,
    )
    return mine.reshape(WHOLE.shape)


def mixed_rows(mixer, part):
    t_hi, t_lo = split(mixer[...])
    lhs = jnp.concatenate([t_hi, t_lo, t_hi, t_lo], axis=1)
    for g in range(0, OWN, 8):
        rows = slice(g, g + 8)
        x = jnp.swapaxes(part[:, rows, :], 0, 1)
        mixed = []
        for i in range(8):
            hi, lo = split(x[i])
            mixed.append(jnp.tanh(dot(lhs, jnp.concatenate([hi, hi, lo, lo], axis=0))))
        yield rows, jnp.stack(mixed)


def mix_kernel(mixer, part, out):
    for rows, mixed in mixed_rows(mixer, part):
        out[:, rows, :] = jnp.swapaxes(mixed, 0, 1)


def mix_weigh_kernel(mixer, weight, part, out):
    w_split = split(weight[...])
    for rows, mixed in mixed_rows(mixer, part):
        done = weigh(mixed.reshape(8 * SNAPS, FEAT), w_split)
        out[:, rows, :] = jnp.swapaxes(done.reshape(8, SNAPS, FEAT), 0, 1)


def mix(mixer, part):
    return call(mix_kernel, "mix", WHOLE, [VSPEC] * 2, [], 1_600_000_000, 4 << 20, mixer, part)


def mix_weigh(mixer, weight, part):
    return call(
        mix_weigh_kernel, "mix_weigh", WHOLE, [VSPEC] * 3, [], 2_400_000_000, 4 << 20, mixer, weight, part
    )


def exchange(x):
    return lax.all_to_all(x, "snap", split_axis=0, concat_axis=0, tiled=True)


def shards(features, tiles, coords, temporal, weight_one, weight_two):
    tiles = tiles.reshape(tiles.shape[1:])
    coords = coords[0].T
    mine = loading_product(coords, features.reshape(VERT, FEAT), tiles, weight_one)
    state = exchange(mix_weigh(temporal, weight_two, exchange(mine)))
    mine = tile_sum(coords, state.reshape(VERT, FEAT), tiles)
    return exchange(mix(temporal, exchange(mine))).reshape(features.shape)


def solution(mesh):
    return jax.shard_map(
        shards,
        mesh=mesh,
        in_specs=(
            P("snap", "rep", None),
            P("snap", "rep", None, None),
            P("snap", "rep", None),
            P(),
            P(),
            P(),
        ),
        out_specs=P("snap", "rep", None),
        check_vma=False,
    )
```

```python
import jax
import jax.numpy as jnp
from jax import lax
from jax.experimental import pallas as pl
from jax.experimental.pallas import tpu as pltpu
from jax.sharding import PartitionSpec as P

SNAPS = 64
VERT, FEAT, TILE = 2048, 256, 128
HALF = FEAT // 2
OWN = VERT // SNAPS
NBLK = VERT // TILE
BF, F32 = jnp.bfloat16, jnp.float32
WHOLE = jax.ShapeDtypeStruct((SNAPS, OWN, FEAT), F32)
PARAMS = pltpu.CompilerParams(vmem_limit_bytes=32 << 20)
MOST = pltpu.CompilerParams(vmem_limit_bytes=60 << 20)
VSPEC = pl.BlockSpec(memory_space=pltpu.VMEM)
SSPEC = pl.BlockSpec(memory_space=pltpu.SMEM)
FAR = pl.BlockSpec(memory_space=pl.ANY)


def split(x):
    hi = x.astype(BF)
    return hi, (x - hi.astype(F32)).astype(BF)


def dot(a, b):
    return jnp.dot(a, b, preferred_element_type=F32)


def put_block(pair, h, blk, value):
    hi, lo = split(value)
    both = jnp.concatenate([hi, lo], axis=1)
    pair[h, blk, :TILE] = both
    pair[h, blk, TILE:] = both


def add_tile(coords, k, tile, pair, acc):
    row = coords[0, k]
    used = row >= 0
    row = jnp.where(used, row, NBLK)
    col = jnp.where(used, coords[1, k], 0)
    lhs = jnp.concatenate(split(tile), axis=1)
    for h in range(2):
        wide = dot(lhs, pair[h, col])
        acc[row, :, h * HALF : (h + 1) * HALF] += wide[:, :HALF] + wide[:, HALF:]


def finish(acc, out):
    out[...] = acc[:NBLK].reshape(SNAPS, OWN, FEAT)


def put_state(state, pair, blk):
    for h in range(2):
        put_block(pair, h, blk, state[blk * TILE : (blk + 1) * TILE, h * HALF : (h + 1) * HALF])


def weigh(rows, w_split):
    w_hi, w_lo = w_split
    s_hi, s_lo = split(rows)
    return dot(s_hi, w_hi) + (dot(s_hi, w_lo) + dot(s_lo, w_hi))


def sum_kernel(coords, state, tiles, out, pair, acc):
    acc[...] = jnp.zeros_like(acc)
    for blk in range(NBLK):
        put_state(state, pair, blk)
    for k in range(tiles.shape[0]):
        add_tile(coords, k, tiles[k], pair, acc)
    finish(acc, out)


def loading_kernel(
    coords_far, state_far, tiles_far, weight_far, out_far, pair, acc, state, tiles, weight, coords, sems
):
    count = tiles.shape[0]
    chunks, step = VERT // CHUNK, count // PIECES
    first = [
        pltpu.make_async_copy(weight_far, weight, sems.at[0]),
        pltpu.make_async_copy(coords_far, coords, sems.at[1]),
    ]
    states = [
        pltpu.make_async_copy(state_far.at[pl.ds(i * CHUNK, CHUNK)], state.at[pl.ds(i * CHUNK, CHUNK)], sems.at[2 + i])
        for i in range(chunks)
    ]
    lists = [
        pltpu.make_async_copy(
            tiles_far.at[pl.ds(i * step, step)], tiles.at[pl.ds(i * step, step)], sems.at[2 + chunks + i]
        )
        for i in range(PIECES)
    ]
    sends = [
        pltpu.make_async_copy(
            state.at[pl.ds(i * CHUNK, CHUNK)], out_far.at[pl.ds(i * CHUNK, CHUNK)], sems.at[2 + chunks + PIECES + i]
        )
        for i in range(chunks)
    ]
    for copy in first + states + lists:
        copy.start()
    acc[...] = jnp.zeros_like(acc)
    for i in range(chunks):
        states[i].wait()
        for blk in range(i * CHUNK // TILE, (i + 1) * CHUNK // TILE):
            put_state(state, pair, blk)
    first[1].wait()
    for i in range(PIECES):
        lists[i].wait()
        for k in range(i * step, (i + 1) * step):
            add_tile(coords, k, tiles[k], pair, acc)
    first[0].wait()
    w_split = split(weight[...])
    for i in range(chunks):
        blks = slice(i * CHUNK // TILE, (i + 1) * CHUNK // TILE)
        state[i * CHUNK : (i + 1) * CHUNK, :] = weigh(acc[blks].reshape(CHUNK, FEAT), w_split)
        sends[i].start()
    for copy in sends:
        copy.wait()


CHUNK, PIECES = 128, 4
SCRATCH = [pltpu.VMEM((2, NBLK, 2 * TILE, FEAT), BF), pltpu.VMEM((NBLK + 1, TILE, FEAT), F32)]


def cost(flops, moved):
    return pl.CostEstimate(flops=flops, bytes_accessed=moved, transcendentals=0)


def call(kernel, name, out_shape, in_specs, scratch, flops, moved, *args, params=PARAMS, out_spec=VSPEC):
    return pl.pallas_call(
        kernel,
        out_shape=out_shape,
        in_specs=in_specs,
        out_specs=out_spec,
        scratch_shapes=scratch,
        compiler_params=params,
        cost_estimate=cost(flops, moved),
        name=name,
    )(*args)


def tile_sum(coords, state, tiles):
    return call(
        sum_kernel, "tile_sum", WHOLE, [SSPEC, VSPEC, VSPEC], SCRATCH,
        1_600_000_000, 6 << 20, coords, state, tiles,
    )


def loading_product(coords, state, tiles, weight):
    near = [pltpu.VMEM(x.shape, F32) for x in (state, tiles, weight)] + [pltpu.SMEM(coords.shape, jnp.int32)]
    sems = [pltpu.SemaphoreType.DMA((2 + 2 * VERT // CHUNK + PIECES,))]
    out = jax.ShapeDtypeStruct((VERT, FEAT), F32)
    mine = call(
        loading_kernel, "loading_product", out, [FAR] * 4, SCRATCH + near + sems,
        3_200_000_000, 6 << 20, coords, state, tiles, weight, params=MOST, out_spec=FAR,
    )
    return mine.reshape(WHOLE.shape)


def mixed_rows(mixer, part):
    t_hi, t_lo = split(mixer[...])
    lhs = jnp.concatenate([t_hi, t_lo, t_hi, t_lo], axis=1)
    for g in range(0, OWN, 8):
        rows = slice(g, g + 8)
        x = jnp.swapaxes(part[:, rows, :], 0, 1)
        mixed = []
        for i in range(8):
            hi, lo = split(x[i])
            mixed.append(jnp.tanh(dot(lhs, jnp.concatenate([hi, hi, lo, lo], axis=0))))
        yield rows, jnp.stack(mixed)


def mix_kernel(mixer, part, out):
    for rows, mixed in mixed_rows(mixer, part):
        out[:, rows, :] = jnp.swapaxes(mixed, 0, 1)


def mix_weigh_kernel(mixer, weight, part, out):
    w_split = split(weight[...])
    for rows, mixed in mixed_rows(mixer, part):
        done = weigh(mixed.reshape(8 * SNAPS, FEAT), w_split)
        out[:, rows, :] = jnp.swapaxes(done.reshape(8, SNAPS, FEAT), 0, 1)


def mix(mixer, part):
    return call(mix_kernel, "mix", WHOLE, [VSPEC] * 2, [], 1_600_000_000, 4 << 20, mixer, part)


def mix_weigh(mixer, weight, part):
    return call(
        mix_weigh_kernel, "mix_weigh", WHOLE, [VSPEC] * 3, [], 2_400_000_000, 4 << 20, mixer, weight, part
    )


def exchange(x):
    return lax.all_to_all(x, "snap", split_axis=0, concat_axis=0, tiled=True)


def shards(features, tiles, coords, temporal, weight_one, weight_two):
    tiles = tiles.reshape(tiles.shape[1:])
    coords = coords[0].T
    mine = loading_product(coords, features.reshape(VERT, FEAT), tiles, weight_one)
    state = exchange(mix_weigh(temporal, weight_two, exchange(mine)))
    mine = tile_sum(coords, state.reshape(VERT, FEAT), tiles)
    return exchange(mix(temporal, exchange(mine))).reshape(features.shape)


def solution(mesh):
    return jax.shard_map(
        shards,
        mesh=mesh,
        in_specs=(
            P("snap", "rep", None),
            P("snap", "rep", None, None),
            P("snap", "rep", None),
            P(),
            P(),
            P(),
        ),
        out_specs=P("snap", "rep", None),
        check_vma=False,
    )
```
